128 devices in a mesh: step: 32 (over y, x, core), seq: 4 (over z).
Axes of the slice: x: 4, y: 4, z: 4, core: 2. Of those that a mesh axis runs over, the one named last changes fastest.
Arguments:
- states: bfloat16 [32, 1024, 1536], P('step', 'seq'), may hold values from -6 to 6
- step_times: int32 [32, 2], P('step'), may hold values from 0 to 999, as said below
- positions: int32 [1024], P('seq'), may hold values from 0 to 1023, each once
- w_qkv: bfloat16 [1536, 4608], replicated, may hold values from -1 to 1
- qk_gain: float32 [2, 1536], replicated, may hold values from 0.2 to 6
- w_out: bfloat16 [1536, 1536], replicated, may hold values from -0.15625 to 0.15625
- time_weight: bfloat16 [256, 4608], replicated, may hold values from -0.375 to 0.375
Outputs:
- drift_sum: float32 [32, 1024, 1536], P('step', 'seq')
The draws below stay inside these ranges and needn't reach their ends.
Inputs may be any that keep to these rules, and one draw needn't show every extreme that they name: `step_times`: column 0 of row k is the timestep index of step k and column 1 that of step k + 1, equal to column 0 of row k + 1; indices fall strictly along the steps and row 0 starts at 999.
All inputs are finite; a program needn't handle non-finite values.
Results may differ from the reference program's by a relative error of at most 0.004.
Values may be sent and summed in bfloat16 or wider, within the bound.
No kernel may reach another device: no remote copies, remote signals or barrier semaphores. Data moves between devices by JAX's collectives and lax.ppermute only.
A program may use at most 192 MiB of HBM per device.

```python
import math
import jax
import jax.numpy as jnp
from jax import lax

D = 1536
HEADS = 12
HEAD = 128
FREQ = 256
SEQ_LEN = 1024
STEPS = 32


def draw_step_times(key, part):
    key = jax.random.fold_in(key, 11)
    gaps = jax.random.randint(key, (STEPS,), 320 // STEPS + 1, 960 // STEPS + 1)
    ends = 999 - jnp.cumsum(gaps)
    starts = ends + gaps
    return jnp.stack([starts, ends], axis=1).astype(jnp.int32)


def draw_qk_gain(key, part):
    key = jax.random.fold_in(key, 12)
    first_key, second_key = jax.random.split(key)
    low_level = math.log(1.0)
    high_level = math.log(2.5)
    head_level = jax.random.uniform(first_key, (2, HEADS, 1), jnp.float32, low_level, high_level)
    channel_level = jax.random.uniform(second_key, (2, HEADS, HEAD), jnp.float32, 0.8, 1.2)
    return (jnp.exp(head_level) * channel_level).reshape(2, D).astype(jnp.float32)


def draw_w_qkv(key, part):
    key = jax.random.fold_in(key, 13)
    matrix_key = jax.random.fold_in(key, 0)
    matrix = jax.random.truncated_normal(matrix_key, -4.0, 4.0, (D, 3 * D), jnp.float32) * D ** (-0.5)
    return matrix.astype(jnp.bfloat16)


def levels(key, dims, pieces, low, largest):
    loudness = 1.0
    for dim, blocks in pieces:
        draws = jax.random.uniform(jax.random.fold_in(jax.random.fold_in(key, 6), dim), (blocks,), jnp.float32, low / len(pieces), largest / len(pieces))
        loudness = loudness * jnp.repeat(jnp.exp(draws), dims[dim] // blocks).reshape((-1,) + (1,) * (len(dims) - 1 - dim))
    return loudness


def noise(key, extent, width, bound, pieces=(), held_as=jnp.bfloat16):
    result = width * jax.random.normal(key, extent, jnp.float32)
    if pieces:
        result = result * levels(key, extent, pieces, -0.22, 0.18)
    return jnp.clip(result, -bound, bound).astype(held_as)


def setup_inputs(seed: int = 0) -> dict:
    key_of = jax.random.split(jax.random.key(seed), 8)
    states = noise(key_of[0], (STEPS, SEQ_LEN, D), 1.0, 6.0, ((0, 32), (1, 4)))
    step_times = draw_step_times(jax.random.fold_in(key_of[7], 71), 0)
    positions = jax.random.permutation(key_of[2], SEQ_LEN).astype(jnp.int32)
    w_qkv = draw_w_qkv(jax.random.fold_in(key_of[7], 71), 0)
    qk_gain = draw_qk_gain(jax.random.fold_in(key_of[7], 71), 0)
    w_out = noise(key_of[5], (D, D), D ** -0.5, 0.15625)
    time_weight = noise(key_of[6], (FREQ, 3 * D), FREQ ** -0.5, 0.375)
    return dict(states=states, step_times=step_times, positions=positions, w_qkv=w_qkv, qk_gain=qk_gain, w_out=w_out, time_weight=time_weight)


epsilon = 1e-06

def rms_norm(entries):
    return entries * lax.rsqrt(lax.optimization_barrier(jnp.mean(entries * entries, axis=-1, keepdims=True)) + epsilon)

def modulation(step_times, time_weight):
    half_width = time_weight.shape[0] // 2
    steps_f = step_times[:, 0].astype(jnp.float32)
    frequency = jnp.exp(-math.log(10000.0) * jnp.arange(half_width, dtype=jnp.float32) / half_width)
    angles = steps_f[:, None] * frequency[None, :]
    embedded = jnp.concatenate([jnp.cos(angles), jnp.sin(angles)], axis=1)
    return jnp.dot(embedded, time_weight.astype(jnp.float32), precision=lax.Precision.HIGHEST)

def rotate(entries, positions):
    half_width = entries.shape[-1] // 2
    inverse = jnp.exp(-math.log(10000.0) * jnp.arange(half_width, dtype=jnp.float32) / half_width)
    angles = positions.astype(jnp.float32)[:, None] * inverse[None, :]
    cosine = jnp.cos(angles)[:, None, :]
    sine_part = jnp.sin(angles)[:, None, :]
    low_half = entries[..., :half_width]
    high_half = entries[..., half_width:]
    return jnp.concatenate([low_half * cosine - high_half * sine_part, low_half * sine_part + high_half * cosine], axis=-1)

def prepare(own_state, positions, shift_mod, scale_mod, w_qkv, qk_gain):
    model_width = own_state.shape[1]
    head_shape = (own_state.shape[0], model_width // HEAD, HEAD)
    normed = (rms_norm(own_state.astype(jnp.float32)) * (1.0 + scale_mod) + shift_mod).astype(jnp.bfloat16)
    projected_qkv = jnp.dot(normed, w_qkv, preferred_element_type=jnp.float32)
    queries = rms_norm(projected_qkv[:, :model_width]) * qk_gain[0]
    key_rows = rms_norm(projected_qkv[:, model_width:2 * model_width]) * qk_gain[1]
    values = projected_qkv[:, 2 * model_width:].reshape(head_shape).astype(jnp.bfloat16)
    queries = rotate(queries.reshape(head_shape), positions).astype(jnp.bfloat16)
    key_rows = rotate(key_rows.reshape(head_shape), positions).astype(jnp.bfloat16)
    return (queries, key_rows, values)

def attend(queries, key_rows, values):
    score_scale = HEAD ** (-0.5)

    def one_head(operands):
        q_head, k_head, v_head = operands
        scores = jnp.dot(q_head, k_head.T, preferred_element_type=jnp.float32) * score_scale
        row_max = lax.optimization_barrier(jnp.max(scores, axis=-1, keepdims=True))
        exp_scores = jnp.exp(scores - row_max)
        row_total = lax.optimization_barrier(jnp.sum(exp_scores, axis=-1, keepdims=True))
        weighted = jnp.dot(exp_scores.astype(jnp.bfloat16), v_head, preferred_element_type=jnp.float32) / row_total
        return weighted.astype(jnp.bfloat16)
    stacked = lax.map(one_head, (queries.transpose(1, 0, 2), key_rows.transpose(1, 0, 2), values.transpose(1, 0, 2)))
    return stacked.transpose(1, 0, 2)

def reference(states, step_times, positions, w_qkv, qk_gain, w_out, time_weight):
    modulations = modulation(step_times, time_weight)

    def one_step(operands):
        own_state, step_pair, modulated = operands
        shift_mod = modulated[:D]
        scale_mod = modulated[D:2 * D]
        gate_mod = modulated[2 * D:]
        queries, key_rows, values = prepare(own_state, positions, shift_mod, scale_mod, w_qkv, qk_gain)
        attended = attend(queries, key_rows, values).reshape(own_state.shape[0], D)
        projected = jnp.dot(attended, w_out, preferred_element_type=jnp.float32)
        velocity = own_state.astype(jnp.float32) + gate_mod * projected
        step_size = (step_pair[1] - step_pair[0]).astype(jnp.float32) / 1000.0
        return step_size * velocity
    drifts = lax.map(one_step, (states, step_times, modulations))
    return jnp.cumsum(drifts, axis=0)
```

```python
import functools
import math

import jax
import jax.numpy as jnp
from jax import lax
from jax.experimental import pallas as pl
from jax.experimental.pallas import tpu as pltpu
from jax.sharding import PartitionSpec as P

D = 1536
HEAD = 128
HEADS = D // HEAD
TILE = 512
TILES = D // TILE
epsilon = 1e-06
EXP_SCALE = HEAD ** (-0.5) * math.log2(math.e)
f32, bf16 = jnp.float32, jnp.bfloat16


def modulation(step_times, time_weight):
    half_width = time_weight.shape[0] // 2
    steps_f = step_times[:, 0].astype(f32)
    frequency = jnp.exp(-math.log(10000.0) * jnp.arange(half_width, dtype=f32) / half_width)
    angles = steps_f[:, None] * frequency[None, :]
    embedded = jnp.concatenate([jnp.cos(angles), jnp.sin(angles)], axis=1)
    return jnp.dot(embedded, time_weight.astype(f32), precision=lax.Precision.HIGHEST)


def rope_tables(positions):
    half_width = HEAD // 2
    inverse = jnp.exp(-math.log(10000.0) * jnp.arange(half_width, dtype=f32) / half_width)
    angles = positions.astype(f32)[:, None] * inverse[None, :]
    cosine, sine = jnp.cos(angles), jnp.sin(angles)
    return jnp.concatenate([cosine, cosine], axis=1), jnp.concatenate([-sine, sine], axis=1)


def norm_rope(proj, gain, cos, sin, out_ref):
    rows = proj.shape[0]
    total = jnp.zeros((rows, HEAD), f32)
    for h in range(HEADS):
        p = proj[:, h * HEAD : (h + 1) * HEAD]
        total = total + p * p
    inv = lax.rsqrt(jnp.sum(total, axis=1, keepdims=True) * (1.0 / D) + epsilon)
    cos, sin = cos[...], sin[...]
    for h in range(HEADS):
        at = slice(h * HEAD, (h + 1) * HEAD)
        y = proj[:, at] * inv * gain[:, at]
        out_ref[:, at] = (y * cos + pltpu.roll(y, HEAD // 2, 1) * sin).astype(bf16)


def project_kernel(n_x, with_q, *refs):
    x_refs, refs = refs[:n_x], refs[n_x:]
    shift, scale, gains, cos, sin, w = refs[:6]
    outs, (normed, proj) = refs[6:-2], refs[-2:]
    i = pl.program_id(0)

    @pl.when(i == 0)
    def _():
        at = 0
        for x_ref in x_refs:
            x = x_ref[...].astype(f32)
            inv = lax.rsqrt(jnp.sum(x * x, axis=1, keepdims=True) * (1.0 / D) + epsilon)
            normed[pl.ds(at, x.shape[0]), :] = (x * inv * (1.0 + scale[...]) + shift[...]).astype(bf16)
            at += x.shape[0]

    acc = jnp.dot(normed[...], w[...], preferred_element_type=f32)
    groups = ["q", "k", "v"] if with_q else ["k", "v"]
    for g, name in enumerate(groups):
        for t in range(TILES):

            @pl.when(i == g * TILES + t)
            def _(g=g, name=name, t=t):
                if name == "v":
                    outs[g][:, t * TILE : (t + 1) * TILE] = acc.astype(bf16)
                else:
                    proj[:, t * TILE : (t + 1) * TILE] = acc
                    if t == TILES - 1:
                        row = 0 if name == "q" else 1
                        norm_rope(proj, gains[row : row + 1, :], cos, sin, outs[g])


def project(xs, shift, scale, gains, cos, sin, w_qkv, with_q):
    rows = sum(x.shape[0] for x in xs)
    groups = 3 if with_q else 2
    first = 0 if with_q else TILES
    whole = lambda a: pl.BlockSpec(a.shape, lambda i: (0, 0))
    small = (shift, scale, gains, cos, sin)
    return pl.pallas_call(
        functools.partial(project_kernel, len(xs), with_q),
        grid=(groups * TILES,),
        in_specs=[whole(x) for x in xs]
        + [whole(a) for a in small]
        + [pl.BlockSpec((D, TILE), lambda i: (0, i + first))],
        out_specs=[pl.BlockSpec((rows, D), lambda i: (0, 0))] * groups,
        out_shape=[jax.ShapeDtypeStruct((rows, D), bf16)] * groups,
        scratch_shapes=[pltpu.VMEM((rows, D), bf16), pltpu.VMEM((rows, D), f32)],
        cost_estimate=pl.CostEstimate(
            flops=2 * rows * D * D * groups, bytes_accessed=2 * D * D * groups, transcendentals=0
        ),
        compiler_params=pltpu.CompilerParams(vmem_limit_bytes=28 << 20),
    )(*xs, *small, w_qkv)


def attend_kernel(n_kv, q_ref, *refs):
    kv, (m_ref, l_ref, acc_ref) = refs[: 2 * n_kv], refs[2 * n_kv :]
    rows = q_ref.shape[0]
    for h in range(HEADS):
        at = slice(h * HEAD, (h + 1) * HEAD)
        q = q_ref[:, at]
        scores = [
            lax.dot_general(q, kv[2 * j][:, at], (((1,), (1,)), ((), ())), preferred_element_type=f32)
            for j in range(n_kv)
        ]
        top = scores[0]
        for s in scores[1:]:
            top = jnp.maximum(top, s)
        m = jnp.max(top, axis=1, keepdims=True) * EXP_SCALE
        total = jnp.zeros((rows, 1), f32)
        acc = jnp.zeros((rows, HEAD), f32)
        for j in range(n_kv):
            p = jnp.exp2(scores[j] * EXP_SCALE - m)
            total = total + jnp.sum(p, axis=1, keepdims=True)
            acc = acc + jnp.dot(p.astype(bf16), kv[2 * j + 1][:, at], preferred_element_type=f32)
        m_ref[:, h : h + 1] = m
        l_ref[:, h : h + 1] = total
        acc_ref[:, at] = acc


def attend(q, kvs):
    rows = q.shape[0]
    keys = sum(k.shape[0] for k, _ in kvs)
    flat = [a for pair in kvs for a in pair]
    vm = pl.BlockSpec(memory_space=pltpu.VMEM)
    return pl.pallas_call(
        functools.partial(attend_kernel, len(kvs)),
        in_specs=[vm] * (1 + len(flat)),
        out_specs=[vm] * 3,
        out_shape=[
            jax.ShapeDtypeStruct((rows, HEAD), f32),
            jax.ShapeDtypeStruct((rows, HEAD), f32),
            jax.ShapeDtypeStruct((rows, D), f32),
        ],
        cost_estimate=pl.CostEstimate(
            flops=8 * rows * D * keys, bytes_accessed=4 * rows * D * 2, transcendentals=rows * keys * HEADS
        ),
        compiler_params=pltpu.CompilerParams(vmem_limit_bytes=28 << 20),
    )(q, *flat)


def finish_kernel(n_kv, h_ref, q_ref, *refs):
    kv, refs = refs[: 2 * n_kv], refs[2 * n_kv :]
    m_ref, l_ref, acc_ref, x_ref, gate_ref, w_hbm, out_ref, w_ref, attended, sem = refs
    load = pltpu.make_async_copy(w_hbm, w_ref, sem)
    load.start()
    for h in range(HEADS):
        at = slice(h * HEAD, (h + 1) * HEAD)
        q = q_ref[:, at]
        scores = [
            lax.dot_general(q, kv[2 * j][:, at], (((1,), (1,)), ((), ())), preferred_element_type=f32)
            for j in range(n_kv)
        ]
        top = scores[0]
        for s in scores[1:]:
            top = jnp.maximum(top, s)
        before = m_ref[:, h : h + 1]
        m = jnp.maximum(jnp.max(top, axis=1, keepdims=True) * EXP_SCALE, before)
        fade = jnp.exp2(before - m)
        total = l_ref[:, h : h + 1] * fade
        acc = acc_ref[:, at] * fade
        for j in range(n_kv):
            p = jnp.exp2(scores[j] * EXP_SCALE - m)
            total = total + jnp.sum(p, axis=1, keepdims=True)
            acc = acc + jnp.dot(p.astype(bf16), kv[2 * j + 1][:, at], preferred_element_type=f32)
        attended[:, at] = (acc / total).astype(bf16)
    load.wait()
    size = h_ref[0, 0]
    for t in range(TILES):
        at = slice(t * TILE, (t + 1) * TILE)
        proj = jnp.dot(attended[...], w_ref[:, at], preferred_element_type=f32)
        out_ref[:, at] = size * (x_ref[:, at].astype(f32) + gate_ref[:, at] * proj)


def finish(step_size, q, kvs, state, x, gate, w_out):
    rows = q.shape[0]
    keys = sum(k.shape[0] for k, _ in kvs)
    flat = [a for pair in kvs for a in pair]
    vm = pl.BlockSpec(memory_space=pltpu.VMEM)
    return pl.pallas_call(
        functools.partial(finish_kernel, len(kvs)),
        in_specs=[pl.BlockSpec(memory_space=pltpu.SMEM)]
        + [vm] * (1 + len(flat) + 3 + 2)
        + [pl.BlockSpec(memory_space=pl.ANY)],
        out_specs=vm,
        out_shape=jax.ShapeDtypeStruct((rows, D), f32),
        scratch_shapes=[pltpu.VMEM((D, D), bf16), pltpu.VMEM((rows, D), bf16), pltpu.SemaphoreType.DMA],
        cost_estimate=pl.CostEstimate(
            flops=8 * rows * D * keys + 2 * rows * D * D,
            bytes_accessed=2 * D * D,
            transcendentals=rows * keys * HEADS,
        ),
        compiler_params=pltpu.CompilerParams(vmem_limit_bytes=28 << 20),
    )(step_size, q, *flat, *state, x, gate, w_out)


def gather_states(x, n):
    half = x.shape[0] // 2
    right = [(i, (i + 1) % n) for i in range(n)]
    left = [(i, (i - 1) % n) for i in range(n)]
    first, second = x[:half], x[half:]
    to_right = lambda v: lax.ppermute(v, "seq", right)
    to_left = lambda v: lax.ppermute(v, "seq", left)
    r_first, l_second = to_right(first), to_left(second)
    r_second, l_first = to_right(second), to_left(first)
    return (r_first, l_second), (r_second, l_first), (to_right(r_first), to_left(l_second))


def scan_steps(inc):
    rows = inc.shape[0]
    half, part = rows // 2, rows // 8
    step = lax.axis_index("step")
    c, xx, yy = step % 2, (step // 2) % 4, step // 8
    pair = [(i, i ^ 1) for i in range(32)]

    def along_x(k):
        return [((y * 4 + x) * 2 + c, (y * 4 + (x + k) % 4) * 2 + c) for y in range(4) for x in range(4) for c in range(2)]

    def along_y(k):
        return [((y * 4 + x) * 2 + c, ((y + k) % 4 * 4 + x) * 2 + c) for y in range(4) for x in range(4) for c in range(2)]

    sent = lax.dynamic_slice_in_dim(inc, (1 - c) * half, half).astype(bf16)
    got = lax.ppermute(sent, "step", pair).astype(f32)
    mine = lax.dynamic_slice_in_dim(inc, c * half, half)
    both = (mine + got).reshape(4, part, D)
    narrow = both.astype(bf16)
    src = [lax.dynamic_index_in_dim(both, xx, 0, keepdims=False)]
    for k in (1, 2, 3):
        piece = lax.dynamic_index_in_dim(narrow, (xx + k) % 4, 0, keepdims=False)
        src.append(lax.ppermute(piece, "step", along_x(k)).astype(f32))
    row = src[0] + src[1] + src[2] + src[3]
    row_b = row.astype(bf16)
    rows_y = [lax.ppermute(row_b, "step", along_y(k)) for k in (1, 2, 3)]
    above = sum(jnp.where((yy - k) % 4 < yy, rows_y[k - 1].astype(f32), 0.0) for k in (1, 2, 3))
    before = []
    for k in range(4):
        target = (xx + k) % 4
        before.append(above + sum(jnp.where((xx - j) % 4 < target, src[j], 0.0) for j in range(4)))
    back = [before[0]] + [lax.ppermute(before[k].astype(bf16), "step", along_x(k)).astype(f32) for k in (1, 2, 3)]
    entering = jnp.zeros((4, part, D), f32)
    for k in range(4):
        entering = lax.dynamic_update_index_in_dim(entering, back[k], (xx - k) % 4, 0)
    entering = entering.reshape(half, D)
    given = jnp.where(c == 0, entering + mine, entering)
    other = lax.ppermute(given.astype(bf16), "step", pair).astype(f32)
    own = jnp.where(c == 0, given, entering + got + mine)
    rest = other + lax.dynamic_slice_in_dim(inc, (1 - c) * half, half)
    return jnp.concatenate([jnp.where(c == 0, own, rest), jnp.where(c == 0, rest, own)])


def on_device(states, step_times, positions, w_qkv, qk_gain, w_out, time_weight):
    n = lax.axis_size("seq")
    z = lax.axis_index("seq")
    x = states[0]
    half = x.shape[0] // 2
    chunks = gather_states(x, n)
    all_positions = lax.all_gather(positions, "seq", axis=0, tiled=True)

    modulated = modulation(step_times, time_weight)
    shift, scale, gate = modulated[:, :D], modulated[:, D : 2 * D], modulated[:, 2 * D :]

    q, k, v = project([x], shift, scale, qk_gain, *rope_tables(positions), w_qkv, True)
    kvs = [(k, v)]
    sources = [((z - 1) % n, (z + 1) % n), ((z - 1) % n, (z + 1) % n), ((z + 2) % n, (z + 2) % n)]
    halves = [(0, 1), (1, 0), (0, 1)]
    for chunk, source, which in zip(chunks, sources, halves):
        where = jnp.concatenate(
            [lax.dynamic_slice_in_dim(all_positions, (2 * s + w) * half, half) for s, w in zip(source, which)]
        )
        kvs.append(tuple(project(chunk, shift, scale, qk_gain, *rope_tables(where), w_qkv, False)))
    state = attend(q, kvs[:3])
    step_size = (step_times[:, 1:] - step_times[:, :1]).astype(f32) / 1000.0
    inc = finish(step_size, q, kvs[3:], state, x, gate, w_out)
    return scan_steps(inc)[None]


def solution(mesh):
    placed = (P("step", "seq", None), P("step", None), P("seq"), P(), P(), P(), P())
    return jax.shard_map(
        on_device, mesh=mesh, in_specs=placed, out_specs=P("step", "seq", None), check_vma=False
    )
```

```python
import functools
import math

import jax
import jax.numpy as jnp
from jax import lax
from jax.experimental import pallas as pl
from jax.experimental.pallas import tpu as pltpu
from jax.sharding import PartitionSpec as P

D = 1536
HEAD = 128
HEADS = D // HEAD
TILE = 512
TILES = D // TILE
WIDE = D + HEAD
VMEM = 16 << 20
epsilon = 1e-06
EXP_SCALE = HEAD ** (-0.5) * math.log2(math.e)
f32, bf16 = jnp.float32, jnp.bfloat16


def modulation(step_times, time_weight):
    half_width = time_weight.shape[0] // 2
    steps_f = step_times[:, 0].astype(f32)
    frequency = jnp.exp(-math.log(10000.0) * jnp.arange(half_width, dtype=f32) / half_width)
    angles = steps_f[:, None] * frequency[None, :]
    embedded = jnp.concatenate([jnp.cos(angles), jnp.sin(angles)], axis=1)
    return jnp.dot(embedded, time_weight.astype(f32), precision=lax.Precision.HIGHEST)


def with_positions(x, positions):
    lane = jnp.arange(HEAD, dtype=jnp.int32)[None, :]
    high, low = (positions // 32)[:, None], (positions % 32)[:, None]
    digits = jnp.where(lane == 0, high, jnp.where(lane == 1, low, 0))
    return jnp.concatenate([x, digits.astype(bf16)], axis=1)


def rope_rates():
    half_width = HEAD // 2
    lane = jnp.arange(HEAD, dtype=jnp.int32)
    inverse = jnp.exp(-math.log(10000.0) * (lane % half_width).astype(f32) / half_width)
    return jnp.stack([inverse, jnp.where(lane < half_width, -1.0, 1.0)])


def norm_rope(proj, gain, cos, sin, out_ref):
    rows = proj.shape[0]
    total = jnp.zeros((rows, HEAD), f32)
    for h in range(HEADS):
        p = proj[:, h * HEAD : (h + 1) * HEAD]
        total = total + p * p
    inv = lax.rsqrt(jnp.sum(total, axis=1, keepdims=True) * (1.0 / D) + epsilon)
    for h in range(HEADS):
        at = slice(h * HEAD, (h + 1) * HEAD)
        y = proj[:, at] * inv * gain[:, at]
        out_ref[:, at] = (y * cos + pltpu.roll(y, HEAD // 2, 1) * sin).astype(bf16)


def project_kernel(with_q, *refs):
    x_refs, (shift, scale, gains, rates, w) = refs[:2], refs[2:7]
    outs, (normed, proj) = refs[7:-2], refs[-2:]
    at, angles = 0, []
    for x_ref in x_refs:
        rows = x_ref.shape[0]
        x = x_ref[:, :D].astype(f32)
        inv = lax.rsqrt(jnp.sum(x * x, axis=1, keepdims=True) * (1.0 / D) + epsilon)
        normed[pl.ds(at, rows), :] = (x * inv * (1.0 + scale[...]) + shift[...]).astype(bf16)
        digits = x_ref[:, D:].astype(f32)
        angles.append((digits[:, 0:1] * 32.0 + digits[:, 1:2]) * rates[0:1, :])
        at += rows
    angles = jnp.concatenate(angles, axis=0)
    cos, sin = jnp.cos(angles), jnp.sin(angles) * rates[1:2, :]
    names = ["q", "k", "v"] if with_q else ["k", "v"]
    out_of = dict(zip(names, outs))
    first = {"q": 0, "k": TILES, "v": 2 * TILES}
    for g, name in enumerate(["k", "q", "v"] if with_q else ["k", "v"]):
        for t in range(TILES):
            at = slice(t * TILE, (t + 1) * TILE)
            col = (first[name] + t) * TILE
            acc = jnp.dot(normed[...], w[:, col : col + TILE], preferred_element_type=f32)
            if name == "v":
                out_of[name][:, at] = acc.astype(bf16)
            else:
                proj[g, :, at] = acc
        if name != "v":
            row = 1 if name == "k" else 0
            norm_rope(proj.at[g], gains[row : row + 1, :], cos, sin, out_of[name])


def project(xs, shift, scale, gains, rates, w_qkv, with_q):
    rows = sum(x.shape[0] for x in xs)
    groups = 3 if with_q else 2
    vm = pl.BlockSpec(memory_space=pltpu.VMEM)
    return pl.pallas_call(
        functools.partial(project_kernel, with_q),
        in_specs=[vm] * 7,
        out_specs=[vm] * groups,
        out_shape=[pltpu.VMEM((rows, D), bf16)] * groups,
        scratch_shapes=[pltpu.VMEM((rows, D), bf16), pltpu.VMEM((groups - 1, rows, D), f32)],
        cost_estimate=pl.CostEstimate(
            flops=2 * rows * D * D * groups, bytes_accessed=2 * D * D * groups, transcendentals=0
        ),
        compiler_params=pltpu.CompilerParams(vmem_limit_bytes=VMEM),
    )(*xs, shift, scale, gains, rates, w_qkv)


def attend_kernel(n_kv, q_ref, *refs):
    kv, (m_ref, l_ref, acc_ref) = refs[: 2 * n_kv], refs[2 * n_kv :]
    rows = q_ref.shape[0]
    for h in range(HEADS):
        at = slice(h * HEAD, (h + 1) * HEAD)
        q = q_ref[:, at]
        scores = [
            lax.dot_general(q, kv[2 * j][:, at], (((1,), (1,)), ((), ())), preferred_element_type=f32)
            for j in range(n_kv)
        ]
        top = scores[0]
        for s in scores[1:]:
            top = jnp.maximum(top, s)
        m = jnp.max(top, axis=1, keepdims=True) * EXP_SCALE
        total = jnp.zeros((rows, 1), f32)
        acc = jnp.zeros((rows, HEAD), f32)
        for j in range(n_kv):
            p = jnp.exp2(scores[j] * EXP_SCALE - m)
            total = total + jnp.sum(p, axis=1, keepdims=True)
            acc = acc + jnp.dot(p.astype(bf16), kv[2 * j + 1][:, at], preferred_element_type=f32)
        m_ref[:, h : h + 1] = m
        l_ref[:, h : h + 1] = total
        acc_ref[:, at] = acc


def attend(q, kvs):
    rows = q.shape[0]
    keys = sum(k.shape[0] for k, _ in kvs)
    flat = [a for pair in kvs for a in pair]
    vm = pl.BlockSpec(memory_space=pltpu.VMEM)
    return pl.pallas_call(
        functools.partial(attend_kernel, len(kvs)),
        in_specs=[vm] * (1 + len(flat)),
        out_specs=[vm] * 3,
        out_shape=[
            pltpu.VMEM((rows, HEAD), f32),
            pltpu.VMEM((rows, HEAD), f32),
            pltpu.VMEM((rows, D), f32),
        ],
        cost_estimate=pl.CostEstimate(
            flops=8 * rows * D * keys, bytes_accessed=4 * rows * D * 2, transcendentals=rows * keys * HEADS
        ),
        compiler_params=pltpu.CompilerParams(vmem_limit_bytes=VMEM),
    )(q, *flat)


def finish_kernel(n_kv, h_ref, q_ref, *refs):
    kv, refs = refs[: 2 * n_kv], refs[2 * n_kv :]
    m_ref, l_ref, acc_ref, x_ref, gate_ref, w_ref, out_ref, attended = refs
    for h in range(HEADS):
        at = slice(h * HEAD, (h + 1) * HEAD)
        q = q_ref[:, at]
        scores = [
            lax.dot_general(q, kv[2 * j][:, at], (((1,), (1,)), ((), ())), preferred_element_type=f32)
            for j in range(n_kv)
        ]
        top = scores[0]
        for s in scores[1:]:
            top = jnp.maximum(top, s)
        before = m_ref[:, h : h + 1]
        m = jnp.maximum(jnp.max(top, axis=1, keepdims=True) * EXP_SCALE, before)
        fade = jnp.exp2(before - m)
        total = l_ref[:, h : h + 1] * fade
        acc = acc_ref[:, at] * fade
        for j in range(n_kv):
            p = jnp.exp2(scores[j] * EXP_SCALE - m)
            total = total + jnp.sum(p, axis=1, keepdims=True)
            acc = acc + jnp.dot(p.astype(bf16), kv[2 * j + 1][:, at], preferred_element_type=f32)
        attended[:, at] = (acc / total).astype(bf16)
    size = h_ref[0, 0]
    for t in range(TILES):
        at = slice(t * TILE, (t + 1) * TILE)
        proj = jnp.dot(attended[...], w_ref[:, at], preferred_element_type=f32)
        out_ref[:, at] = size * (x_ref[:, at].astype(f32) + gate_ref[:, at] * proj)


def finish(step_size, q, kvs, state, x, gate, w_out):
    rows = q.shape[0]
    keys = sum(k.shape[0] for k, _ in kvs)
    flat = [a for pair in kvs for a in pair]
    vm = pl.BlockSpec(memory_space=pltpu.VMEM)
    return pl.pallas_call(
        functools.partial(finish_kernel, len(kvs)),
        in_specs=[pl.BlockSpec(memory_space=pltpu.SMEM)]
        + [vm] * (1 + len(flat) + 3 + 3),
        out_specs=vm,
        out_shape=pltpu.VMEM((rows, D), f32),
        scratch_shapes=[pltpu.VMEM((rows, D), bf16)],
        cost_estimate=pl.CostEstimate(
            flops=8 * rows * D * keys + 2 * rows * D * D,
            bytes_accessed=2 * D * D,
            transcendentals=rows * keys * HEADS,
        ),
        compiler_params=pltpu.CompilerParams(vmem_limit_bytes=VMEM),
    )(step_size, q, *flat, *state, x, gate, w_out)


def gather_states(first, second, n):
    right = [(i, (i + 1) % n) for i in range(n)]
    left = [(i, (i - 1) % n) for i in range(n)]
    to_right = lambda v: lax.ppermute(v, "seq", right)
    to_left = lambda v: lax.ppermute(v, "seq", left)
    r_first, l_second = to_right(first), to_left(second)
    r_second, l_first = to_right(second), to_left(first)
    return (r_first, l_second), (r_second, l_first), (to_right(r_first), to_left(l_second))


def scan_steps(inc):
    rows = inc.shape[0]
    half, part = rows // 2, rows // 8
    step = lax.axis_index("step")
    c, xx, yy = step % 2, (step // 2) % 4, step // 8
    pair = [(i, i ^ 1) for i in range(32)]

    def along_x(k):
        return [((y * 4 + x) * 2 + c, (y * 4 + (x + k) % 4) * 2 + c) for y in range(4) for x in range(4) for c in range(2)]

    def along_y(k):
        return [((y * 4 + x) * 2 + c, ((y + k) % 4 * 4 + x) * 2 + c) for y in range(4) for x in range(4) for c in range(2)]

    sent = lax.dynamic_slice_in_dim(inc, (1 - c) * half, half).astype(bf16)
    got = lax.ppermute(sent, "step", pair).astype(f32)
    mine = lax.dynamic_slice_in_dim(inc, c * half, half)
    both = (mine + got).reshape(4, part, D)
    narrow = both.astype(bf16)
    src = [lax.dynamic_index_in_dim(both, xx, 0, keepdims=False)]
    for k in (1, 2, 3):
        piece = lax.dynamic_index_in_dim(narrow, (xx + k) % 4, 0, keepdims=False)
        src.append(lax.ppermute(piece, "step", along_x(k)).astype(f32))
    row = src[0] + src[1] + src[2] + src[3]
    row_b = row.astype(bf16)
    rows_y = [lax.ppermute(row_b, "step", along_y(k)) for k in (1, 2, 3)]
    above = sum(jnp.where((yy - k) % 4 < yy, rows_y[k - 1].astype(f32), 0.0) for k in (1, 2, 3))
    before = []
    for k in range(4):
        target = (xx + k) % 4
        before.append(above + sum(jnp.where((xx - j) % 4 < target, src[j], 0.0) for j in range(4)))
    back = [before[0]] + [lax.ppermute(before[k].astype(bf16), "step", along_x(k)).astype(f32) for k in (1, 2, 3)]
    entering = jnp.zeros((4, part, D), f32)
    for k in range(4):
        entering = lax.dynamic_update_index_in_dim(entering, back[k], (xx - k) % 4, 0)
    entering = entering.reshape(half, D)
    given = jnp.where(c == 0, entering + mine, entering)
    other = lax.ppermute(given.astype(bf16), "step", pair).astype(f32)
    own = jnp.where(c == 0, given, entering + got + mine)
    rest = other + lax.dynamic_slice_in_dim(inc, (1 - c) * half, half)
    return jnp.concatenate([jnp.where(c == 0, own, rest), jnp.where(c == 0, rest, own)])


def on_device(states, step_times, positions, w_qkv, qk_gain, w_out, time_weight):
    n = lax.axis_size("seq")
    x = states[0]
    half = x.shape[0] // 2
    message = with_positions(x, positions)
    own = (message[:half], message[half:])
    chunks = gather_states(*own, n)

    modulated = modulation(step_times, time_weight)
    shift, scale, gate = modulated[:, :D], modulated[:, D : 2 * D], modulated[:, 2 * D :]
    rates = rope_rates()

    q, k, v = project(own, shift, scale, qk_gain, rates, w_qkv, True)
    kvs = [(k, v)]
    for chunk in chunks:
        kvs.append(tuple(project(chunk, shift, scale, qk_gain, rates, w_qkv, False)))
    state = attend(q, kvs[:3])
    step_size = (step_times[:, 1:] - step_times[:, :1]).astype(f32) / 1000.0
    inc = finish(step_size, q, kvs[3:], state, x, gate, w_out)
    return scan_steps(inc)[None]


def solution(mesh):
    placed = (P("step", "seq", None), P("step", None), P("seq"), P(), P(), P(), P())
    return jax.shard_map(
        on_device, mesh=mesh, in_specs=placed, out_specs=P("step", "seq", None), check_vma=False
    )
```

```python
import functools
import math

import jax
import jax.numpy as jnp
from jax import lax
from jax.experimental import pallas as pl
from jax.experimental.pallas import tpu as pltpu
from jax.sharding import PartitionSpec as P

D = 1536
HEAD = 128
HEADS = D // HEAD
TILE = 512
TILES = D // TILE
WIDE = D + HEAD
VMEM = 16 << 20
epsilon = 1e-06
EXP_SCALE = HEAD ** (-0.5) * math.log2(math.e)
f32, bf16 = jnp.float32, jnp.bfloat16


def modulation(step_times, time_weight):
    half_width = time_weight.shape[0] // 2
    steps_f = step_times[:, 0].astype(f32)
    frequency = jnp.exp(-math.log(10000.0) * jnp.arange(half_width, dtype=f32) / half_width)
    angles = steps_f[:, None] * frequency[None, :]
    embedded = jnp.concatenate([jnp.cos(angles), jnp.sin(angles)], axis=1)
    return jnp.dot(embedded, time_weight.astype(f32), precision=lax.Precision.HIGHEST)


def message_kernel(x_ref, positions_ref, first_ref, second_ref):
    rows = first_ref.shape[0]
    lane = lax.broadcasted_iota(jnp.int32, (rows, HEAD), 1)
    for at, out in ((0, first_ref), (rows, second_ref)):
        ids = positions_ref[at : at + rows, :]
        out[:, :D] = x_ref[at : at + rows, :]
        out[:, D:] = jnp.where(lane == 0, ids >> 5, jnp.where(lane == 1, ids & 31, 0)).astype(f32).astype(bf16)


def with_positions(x, positions):
    half = x.shape[0] // 2
    vm = pl.BlockSpec(memory_space=pltpu.VMEM)
    return pl.pallas_call(
        message_kernel,
        in_specs=[vm] * 2,
        out_specs=[vm] * 2,
        out_shape=[pltpu.VMEM((half, WIDE), bf16)] * 2,
        compiler_params=pltpu.CompilerParams(vmem_limit_bytes=4 << 20),
    )(x, positions[:, None])


def rope_rates():
    half_width = HEAD // 2
    lane = jnp.arange(HEAD, dtype=jnp.int32)
    inverse = jnp.exp(-math.log(10000.0) * (lane % half_width).astype(f32) / half_width)
    return jnp.stack([inverse, jnp.where(lane < half_width, -1.0, 1.0)])


def norm_rope(proj, gain, cos, sin, out_ref):
    rows = proj.shape[0]
    total = jnp.zeros((rows, HEAD), f32)
    for h in range(HEADS):
        p = proj[:, h * HEAD : (h + 1) * HEAD]
        total = total + p * p
    inv = lax.rsqrt(jnp.sum(total, axis=1, keepdims=True) * (1.0 / D) + epsilon)
    for h in range(HEADS):
        at = slice(h * HEAD, (h + 1) * HEAD)
        y = proj[:, at] * inv * gain[:, at]
        out_ref[:, at] = (y * cos + pltpu.roll(y, HEAD // 2, 1) * sin).astype(bf16)


def project_kernel(with_q, *refs):
    x_refs, (shift, scale, gains, rates, w) = refs[:2], refs[2:7]
    outs, (normed, proj) = refs[7:-2], refs[-2:]
    at, angles = 0, []
    for x_ref in x_refs:
        rows = x_ref.shape[0]
        x = x_ref[:, :D].astype(f32)
        inv = lax.rsqrt(jnp.sum(x * x, axis=1, keepdims=True) * (1.0 / D) + epsilon)
        normed[pl.ds(at, rows), :] = (x * inv * (1.0 + scale[...]) + shift[...]).astype(bf16)
        digits = x_ref[:, D:].astype(f32)
        angles.append((digits[:, 0:1] * 32.0 + digits[:, 1:2]) * rates[0:1, :])
        at += rows
    angles = jnp.concatenate(angles, axis=0)
    cos, sin = jnp.cos(angles), jnp.sin(angles) * rates[1:2, :]
    names = ["q", "k", "v"] if with_q else ["k", "v"]
    out_of = dict(zip(names, outs))
    first = {"q": 0, "k": TILES, "v": 2 * TILES}
    for g, name in enumerate(["k", "q", "v"] if with_q else ["k", "v"]):
        for t in range(TILES):
            at = slice(t * TILE, (t + 1) * TILE)
            col = (first[name] + t) * TILE
            acc = jnp.dot(normed[...], w[:, col : col + TILE], preferred_element_type=f32)
            if name == "v":
                out_of[name][:, at] = acc.astype(bf16)
            else:
                proj[g, :, at] = acc
        if name != "v":
            row = 1 if name == "k" else 0
            norm_rope(proj.at[g], gains[row : row + 1, :], cos, sin, out_of[name])


def project(xs, shift, scale, gains, rates, w_qkv, with_q):
    rows = sum(x.shape[0] for x in xs)
    groups = 3 if with_q else 2
    vm = pl.BlockSpec(memory_space=pltpu.VMEM)
    return pl.pallas_call(
        functools.partial(project_kernel, with_q),
        in_specs=[vm] * 7,
        out_specs=[vm] * groups,
        out_shape=[pltpu.VMEM((rows, D), bf16)] * groups,
        scratch_shapes=[pltpu.VMEM((rows, D), bf16), pltpu.VMEM((groups - 1, rows, D), f32)],
        cost_estimate=pl.CostEstimate(
            flops=2 * rows * D * D * groups, bytes_accessed=2 * D * D * groups, transcendentals=0
        ),
        compiler_params=pltpu.CompilerParams(vmem_limit_bytes=8 << 20),
    )(*xs, shift, scale, gains, rates, w_qkv)


def attend_kernel(n_kv, q_ref, *refs):
    kv, (m_ref, l_ref, acc_ref) = refs[: 2 * n_kv], refs[2 * n_kv :]
    rows = q_ref.shape[0]
    for h in range(HEADS):
        at = slice(h * HEAD, (h + 1) * HEAD)
        q = q_ref[:, at]
        scores = [
            lax.dot_general(q, kv[2 * j][:, at], (((1,), (1,)), ((), ())), preferred_element_type=f32)
            for j in range(n_kv)
        ]
        top = scores[0]
        for s in scores[1:]:
            top = jnp.maximum(top, s)
        m = jnp.max(top, axis=1, keepdims=True) * EXP_SCALE
        total = jnp.zeros((rows, 1), f32)
        acc = jnp.zeros((rows, HEAD), f32)
        for j in range(n_kv):
            p = jnp.exp2(scores[j] * EXP_SCALE - m)
            total = total + jnp.sum(p, axis=1, keepdims=True)
            acc = acc + jnp.dot(p.astype(bf16), kv[2 * j + 1][:, at], preferred_element_type=f32)
        m_ref[:, h : h + 1] = m
        l_ref[:, h : h + 1] = total
        acc_ref[:, at] = acc


def attend(q, kvs):
    rows = q.shape[0]
    keys = sum(k.shape[0] for k, _ in kvs)
    flat = [a for pair in kvs for a in pair]
    vm = pl.BlockSpec(memory_space=pltpu.VMEM)
    return pl.pallas_call(
        functools.partial(attend_kernel, len(kvs)),
        in_specs=[vm] * (1 + len(flat)),
        out_specs=[vm] * 3,
        out_shape=[
            pltpu.VMEM((rows, HEAD), f32),
            pltpu.VMEM((rows, HEAD), f32),
            pltpu.VMEM((rows, D), f32),
        ],
        cost_estimate=pl.CostEstimate(
            flops=8 * rows * D * keys, bytes_accessed=4 * rows * D * 2, transcendentals=rows * keys * HEADS
        ),
        compiler_params=pltpu.CompilerParams(vmem_limit_bytes=10 << 20),
    )(q, *flat)


def finish_kernel(n_kv, h_ref, place_ref, q_ref, *refs):
    kv, refs = refs[: 2 * n_kv], refs[2 * n_kv :]
    m_ref, l_ref, acc_ref, x_ref, gate_ref, w_ref, out_ref, sent_ref, attended = refs
    for h in range(HEADS):
        at = slice(h * HEAD, (h + 1) * HEAD)
        q = q_ref[:, at]
        scores = [
            lax.dot_general(q, kv[2 * j][:, at], (((1,), (1,)), ((), ())), preferred_element_type=f32)
            for j in range(n_kv)
        ]
        top = scores[0]
        for s in scores[1:]:
            top = jnp.maximum(top, s)
        before = m_ref[:, h : h + 1]
        m = jnp.maximum(jnp.max(top, axis=1, keepdims=True) * EXP_SCALE, before)
        fade = jnp.exp2(before - m)
        total = l_ref[:, h : h + 1] * fade
        acc = acc_ref[:, at] * fade
        for j in range(n_kv):
            p = jnp.exp2(scores[j] * EXP_SCALE - m)
            total = total + jnp.sum(p, axis=1, keepdims=True)
            acc = acc + jnp.dot(p.astype(bf16), kv[2 * j + 1][:, at], preferred_element_type=f32)
        attended[:, at] = (acc / total).astype(bf16)
    size = h_ref[0, 0]
    for t in range(TILES):
        at = slice(t * TILE, (t + 1) * TILE)
        proj = jnp.dot(attended[...], w_ref[:, at], preferred_element_type=f32)
        out_ref[:, at] = size * (x_ref[:, at].astype(f32) + gate_ref[:, at] * proj)
    half = sent_ref.shape[0]
    theirs = pl.ds(pl.multiple_of((1 - place_ref[0]) * half, half), half)
    sent_ref[...] = out_ref[theirs, :].astype(bf16)


def finish(step_size, place, q, kvs, state, x, gate, w_out):
    rows = q.shape[0]
    keys = sum(k.shape[0] for k, _ in kvs)
    flat = [a for pair in kvs for a in pair]
    vm = pl.BlockSpec(memory_space=pltpu.VMEM)
    return pl.pallas_call(
        functools.partial(finish_kernel, len(kvs)),
        in_specs=[pl.BlockSpec(memory_space=pltpu.SMEM)] * 2
        + [vm] * (1 + len(flat) + 3 + 3),
        out_specs=[vm] * 2,
        out_shape=[pltpu.VMEM((rows, D), f32), pltpu.VMEM((rows // 2, D), bf16)],
        scratch_shapes=[pltpu.VMEM((rows, D), bf16)],
        cost_estimate=pl.CostEstimate(
            flops=8 * rows * D * keys + 2 * rows * D * D,
            bytes_accessed=2 * D * D,
            transcendentals=rows * keys * HEADS,
        ),
        compiler_params=pltpu.CompilerParams(vmem_limit_bytes=6 << 20),
    )(step_size, place, q, *flat, *state, x, gate, w_out)


def split_kernel(place, inc, got, own, *pieces):
    c, xx = place[0], place[1]
    part = own.shape[0]
    for k, out in enumerate((own,) + pieces):
        at = pl.multiple_of(((xx + k) & 3) * part, part)
        both = inc[pl.ds(pl.multiple_of(c * 4 * part, part) + at, part), :] + got[pl.ds(at, part), :].astype(f32)
        out[...] = both.astype(out.dtype)


def row_kernel(own, one, two, three, out):
    out[...] = (own[...] + one[...].astype(f32) + two[...].astype(f32) + three[...].astype(f32)).astype(bf16)


def before_kernel(place, own, *refs):
    xs, ys, outs = refs[:3], refs[3:6], refs[6:]
    xx, yy = place[1], place[2]
    above = jnp.zeros(own.shape, f32)
    for k in (1, 2, 3):
        above = above + jnp.where(((yy - k) & 3) < yy, ys[k - 1][...].astype(f32), 0.0)
    src = [own[...]] + [r[...].astype(f32) for r in xs]
    for k, out in enumerate(outs):
        total = above
        for j in range(4):
            total = total + jnp.where(((xx - j) & 3) < ((xx + k) & 3), src[j], 0.0)
        out[...] = total.astype(out.dtype)


def join_kernel(place, inc, got, *refs):
    pieces, (own, given) = refs[:4], refs[4:]
    c, xx = place[0], place[1]
    part = pieces[0].shape[0]
    for k in range(4):
        at = pl.multiple_of(((xx - k) & 3) * part, part)
        mine = inc[pl.ds(pl.multiple_of(c * 4 * part, part) + at, part), :]
        theirs = got[pl.ds(at, part), :].astype(f32)
        entering = pieces[k][...].astype(f32)
        even = entering + jnp.where(c == 0, mine, theirs)
        own[pl.ds(at, part), :] = jnp.where(c == 0, even, even + mine)
        given[pl.ds(at, part), :] = jnp.where(c == 0, even, entering).astype(bf16)


def last_kernel(place, inc, own, other, out):
    c, half = place[0], own.shape[0]
    at = pl.multiple_of(c * half, half)
    rest = pl.multiple_of((1 - c) * half, half)
    out[pl.ds(at, half), :] = own[...]
    out[pl.ds(rest, half), :] = other[...].astype(f32) + inc[pl.ds(rest, half), :]


def small_call(kernel, place, args, outs):
    vm = pl.BlockSpec(memory_space=pltpu.VMEM)
    head = [] if place is None else [place]
    return pl.pallas_call(
        kernel,
        in_specs=[pl.BlockSpec(memory_space=pltpu.SMEM)] * len(head) + [vm] * len(args),
        out_specs=[vm] * len(outs),
        out_shape=outs,
        compiler_params=pltpu.CompilerParams(vmem_limit_bytes=3 << 20),
    )(*head, *args)


def scan_steps(place, inc, sent):
    rows = inc.shape[0]
    half, part = rows // 2, rows // 8
    pair = [(i, i ^ 1) for i in range(32)]
    ring = range(4)

    def along_x(k):
        return [((y * 4 + x) * 2 + c, (y * 4 + (x + k) % 4) * 2 + c) for y in ring for x in ring for c in (0, 1)]

    def along_y(k):
        return [((y * 4 + x) * 2 + c, ((y + k) % 4 * 4 + x) * 2 + c) for y in ring for x in ring for c in (0, 1)]

    narrow, wide = pltpu.VMEM((part, D), bf16), pltpu.VMEM((part, D), f32)
    got = lax.ppermute(sent, "step", pair)
    own, *pieces = small_call(split_kernel, place, (inc, got), [wide] + [narrow] * 3)
    xs = [lax.ppermute(piece, "step", along_x(k)) for k, piece in zip((1, 2, 3), pieces)]
    (row,) = small_call(row_kernel, None, (own, *xs), [narrow])
    ys = [lax.ppermute(row, "step", along_y(k)) for k in (1, 2, 3)]
    home, *away = small_call(before_kernel, place, (own, *xs, *ys), [wide] + [narrow] * 3)
    back = [lax.ppermute(piece, "step", along_x(k)) for k, piece in zip((1, 2, 3), away)]
    done, given = small_call(
        join_kernel, place, (inc, got, home, *back), [pltpu.VMEM((half, D), f32), pltpu.VMEM((half, D), bf16)]
    )
    other = lax.ppermute(given, "step", pair)
    return small_call(last_kernel, place, (inc, done, other), [jax.ShapeDtypeStruct((rows, D), f32)])[0]


def on_device(states, step_times, positions, w_qkv, qk_gain, w_out, time_weight):
    n = lax.axis_size("seq")
    right = [(i, (i + 1) % n) for i in range(n)]
    left = [(i, (i - 1) % n) for i in range(n)]
    to_right = lambda v: lax.ppermute(v, "seq", right)
    to_left = lambda v: lax.ppermute(v, "seq", left)
    step = lax.axis_index("step")
    place = jnp.stack([step % 2, (step // 2) % 4, step // 8])

    x = states[0]
    first, second = with_positions(x, positions)
    r_first, l_second = to_right(first), to_left(second)
    step_size = (step_times[:, 1:] - step_times[:, :1]).astype(f32) / 1000.0
    ready = (modulation(step_times, time_weight), rope_rates(), step_size, place, second, first)
    modulated, rates, step_size, place, second_later, first_later = lax.optimization_barrier(ready)
    r_second, l_first = to_right(second_later), to_left(first_later)
    forward = to_right(r_first), to_left(l_second)
    shift, scale, gate = modulated[:, :D], modulated[:, D : 2 * D], modulated[:, 2 * D :]

    q, k, v = project((first_later, second_later), shift, scale, qk_gain, rates, w_qkv, True)
    kvs = [(k, v)]
    for chunk in ((r_first, l_second), (r_second, l_first), forward):
        kvs.append(tuple(project(chunk, shift, scale, qk_gain, rates, w_qkv, False)))
    state = attend(q, kvs[:3])
    inc, sent = finish(step_size, place, q, kvs[3:], state, x, gate, w_out)
    return scan_steps(place, inc, sent)[None]


def solution(mesh):
    placed = (P("step", "seq", None), P("step", None), P("seq"), P(), P(), P(), P())
    return jax.shard_map(
        on_device, mesh=mesh, in_specs=placed, out_specs=P("step", "seq", None), check_vma=False
    )
```

```python
import functools
import math

import jax
import jax.numpy as jnp
from jax import lax
from jax.experimental import pallas as pl
from jax.experimental.pallas import tpu as pltpu
from jax.sharding import PartitionSpec as P

D = 1536
HEAD = 128
HEADS = D // HEAD
TILE = 512
TILES = D // TILE
HINT = 1 << 33
WIDE = D + HEAD
VMEM = 16 << 20
epsilon = 1e-06
EXP_SCALE = HEAD ** (-0.5) * math.log2(math.e)
f32, bf16 = jnp.float32, jnp.bfloat16


def modulation_kernel(times, weight, shift, scale, gate, rates):
    rows, freq = 16, HEAD
    lane = lax.broadcasted_iota(jnp.int32, (rows, freq), 1)
    row = lax.broadcasted_iota(jnp.int32, (rows, 2 * freq), 0)
    t = jnp.full((rows, freq), times[0, 0], jnp.int32).astype(f32)
    angles = t * jnp.exp(-math.log(10000.0) * lane.astype(f32) / freq)
    embedded = jnp.concatenate([jnp.cos(angles), jnp.sin(angles)], axis=1)
    high = embedded.astype(bf16).astype(f32)
    middle = (embedded - high).astype(bf16).astype(f32)
    low = embedded - high - middle
    terms = jnp.where(row == 0, high, jnp.where(row == 1, middle, jnp.where(row == 2, low, 0.0))).astype(bf16)
    for g, out in enumerate((shift, scale, gate)):
        product = jnp.dot(terms, weight[:, g * D : (g + 1) * D], preferred_element_type=f32)
        out[...] = jnp.sum(product, axis=0, keepdims=True)
    half_width = HEAD // 2
    lane = lax.broadcasted_iota(jnp.int32, (1, HEAD), 1)
    rates[0:1, :] = jnp.exp(-math.log(10000.0) * (lane & (half_width - 1)).astype(f32) / half_width)
    rates[1:2, :] = jnp.where(lane < half_width, -1.0, 1.0)


def modulation(step_times, time_weight):
    vm = pl.BlockSpec(memory_space=pltpu.VMEM)
    return pl.pallas_call(
        modulation_kernel,
        in_specs=[pl.BlockSpec(memory_space=pltpu.SMEM), vm],
        out_specs=[vm] * 4,
        out_shape=[pltpu.VMEM((1, D), f32)] * 3 + [pltpu.VMEM((2, HEAD), f32)],
        cost_estimate=pl.CostEstimate(flops=HINT, bytes_accessed=0, transcendentals=0),
        compiler_params=pltpu.CompilerParams(vmem_limit_bytes=3 << 20),
    )(step_times, time_weight)


def message_kernel(x, positions, first, second, sems):
    rows = first.shape[0]
    loads = [
        pltpu.make_async_copy(x.at[pl.ds(j * rows, rows), :], out.at[:, pl.ds(0, D)], sems.at[j])
        for j, out in enumerate((first, second))
    ]
    for load in loads:
        load.start()
    lane = lax.broadcasted_iota(jnp.int32, (rows, HEAD), 1)
    row = lax.broadcasted_iota(jnp.int32, (rows, HEAD), 0)
    for j, out in enumerate((first, second)):
        spread = jnp.where(row == lane, positions[j : j + 1, :], 0).astype(f32)
        ids = jnp.sum(spread, axis=1, keepdims=True).astype(jnp.int32)
        out[:, D:] = jnp.where(lane == 0, ids >> 5, jnp.where(lane == 1, ids & 31, 0)).astype(f32).astype(bf16)
    for load in loads:
        load.wait()


def with_positions(x, positions):
    half = x.shape[0] // 2
    vm = pl.BlockSpec(memory_space=pltpu.VMEM)
    return pl.pallas_call(
        message_kernel,
        in_specs=[pl.BlockSpec(memory_space=pl.ANY), vm],
        out_specs=[vm] * 2,
        out_shape=[pltpu.VMEM((half, WIDE), bf16)] * 2,
        scratch_shapes=[pltpu.SemaphoreType.DMA((2,))],
        cost_estimate=pl.CostEstimate(flops=HINT, bytes_accessed=0, transcendentals=0),
        compiler_params=pltpu.CompilerParams(vmem_limit_bytes=4 << 20),
    )(x, positions.reshape(2, half))


def norm_rope(proj, gain, cos, sin, out_ref):
    rows = proj.shape[0]
    total = jnp.zeros((rows, HEAD), f32)
    for h in range(HEADS):
        p = proj[:, h * HEAD : (h + 1) * HEAD]
        total = total + p * p
    inv = lax.rsqrt(jnp.sum(total, axis=1, keepdims=True) * (1.0 / D) + epsilon)
    for h in range(HEADS):
        at = slice(h * HEAD, (h + 1) * HEAD)
        y = proj[:, at] * inv * gain[:, at]
        out_ref[:, at] = (y * cos + pltpu.roll(y, HEAD // 2, 1) * sin).astype(bf16)


def project_kernel(with_q, *refs):
    x_refs, (shift, scale, gains, rates, w) = refs[:2], refs[2:7]
    outs, (normed, proj) = refs[7:-2], refs[-2:]
    at, angles = 0, []
    for x_ref in x_refs:
        rows = x_ref.shape[0]
        x = x_ref[:, :D].astype(f32)
        inv = lax.rsqrt(jnp.sum(x * x, axis=1, keepdims=True) * (1.0 / D) + epsilon)
        normed[pl.ds(at, rows), :] = (x * inv * (1.0 + scale[...]) + shift[...]).astype(bf16)
        digits = x_ref[:, D:].astype(f32)
        angles.append((digits[:, 0:1] * 32.0 + digits[:, 1:2]) * rates[0:1, :])
        at += rows
    angles = jnp.concatenate(angles, axis=0)
    cos, sin = jnp.cos(angles), jnp.sin(angles) * rates[1:2, :]
    names = ["q", "k", "v"] if with_q else ["k", "v"]
    out_of = dict(zip(names, outs))
    first = {"q": 0, "k": TILES, "v": 2 * TILES}
    for g, name in enumerate(["k", "q", "v"] if with_q else ["k", "v"]):
        for t in range(TILES):
            at = slice(t * TILE, (t + 1) * TILE)
            col = (first[name] + t) * TILE
            acc = jnp.dot(normed[...], w[:, col : col + TILE], preferred_element_type=f32)
            if name == "v":
                out_of[name][:, at] = acc.astype(bf16)
            else:
                proj[g, :, at] = acc
        if name != "v":
            row = 1 if name == "k" else 0
            norm_rope(proj.at[g], gains[row : row + 1, :], cos, sin, out_of[name])


def project(xs, shift, scale, gains, rates, w_qkv, with_q):
    rows = sum(x.shape[0] for x in xs)
    groups = 3 if with_q else 2
    vm = pl.BlockSpec(memory_space=pltpu.VMEM)
    return pl.pallas_call(
        functools.partial(project_kernel, with_q),
        in_specs=[vm] * 7,
        out_specs=[vm] * groups,
        out_shape=[pltpu.VMEM((rows, D), bf16)] * groups,
        scratch_shapes=[pltpu.VMEM((rows, D), bf16), pltpu.VMEM((groups - 1, rows, D), f32)],
        cost_estimate=pl.CostEstimate(
            flops=2 * rows * D * D * groups, bytes_accessed=2 * D * D * groups, transcendentals=0
        ),
        compiler_params=pltpu.CompilerParams(vmem_limit_bytes=8 << 20),
    )(*xs, shift, scale, gains, rates, w_qkv)


def attend_kernel(n_kv, q_ref, *refs):
    kv, (m_ref, l_ref, acc_ref) = refs[: 2 * n_kv], refs[2 * n_kv :]
    rows = q_ref.shape[0]
    for h in range(HEADS):
        at = slice(h * HEAD, (h + 1) * HEAD)
        q = q_ref[:, at]
        scores = [
            lax.dot_general(q, kv[2 * j][:, at], (((1,), (1,)), ((), ())), preferred_element_type=f32)
            for j in range(n_kv)
        ]
        top = scores[0]
        for s in scores[1:]:
            top = jnp.maximum(top, s)
        m = jnp.max(top, axis=1, keepdims=True) * EXP_SCALE
        total = jnp.zeros((rows, 1), f32)
        acc = jnp.zeros((rows, HEAD), f32)
        for j in range(n_kv):
            p = jnp.exp2(scores[j] * EXP_SCALE - m)
            total = total + jnp.sum(p, axis=1, keepdims=True)
            acc = acc + jnp.dot(p.astype(bf16), kv[2 * j + 1][:, at], preferred_element_type=f32)
        m_ref[h] = jnp.broadcast_to(m, (rows, HEAD))
        l_ref[h] = jnp.broadcast_to(total, (rows, HEAD))
        acc_ref[:, at] = acc


def attend(q, kvs):
    rows = q.shape[0]
    keys = sum(k.shape[0] for k, _ in kvs)
    flat = [a for pair in kvs for a in pair]
    vm = pl.BlockSpec(memory_space=pltpu.VMEM)
    return pl.pallas_call(
        functools.partial(attend_kernel, len(kvs)),
        in_specs=[vm] * (1 + len(flat)),
        out_specs=[vm] * 3,
        out_shape=[
            pltpu.VMEM((HEADS, rows, HEAD), f32),
            pltpu.VMEM((HEADS, rows, HEAD), f32),
            pltpu.VMEM((rows, D), f32),
        ],
        cost_estimate=pl.CostEstimate(
            flops=8 * rows * D * keys, bytes_accessed=4 * rows * D * 2, transcendentals=rows * keys * HEADS
        ),
        compiler_params=pltpu.CompilerParams(vmem_limit_bytes=12 << 20),
    )(q, *flat)


def finish_kernel(n_kv, h_ref, place_ref, q_ref, *refs):
    kv, refs = refs[: 2 * n_kv], refs[2 * n_kv :]
    m_ref, l_ref, acc_ref, x_ref, gate_ref, w_ref, out_ref, sent_ref, attended = refs
    rows = q_ref.shape[0]
    for h in range(HEADS):
        at = slice(h * HEAD, (h + 1) * HEAD)
        q = q_ref[:, at]
        scores = [
            lax.dot_general(q, kv[2 * j][:, at], (((1,), (1,)), ((), ())), preferred_element_type=f32)
            for j in range(n_kv)
        ]
        top = scores[0]
        for s in scores[1:]:
            top = jnp.maximum(top, s)
        new = jnp.max(top, axis=1, keepdims=True) * EXP_SCALE
        total = jnp.zeros((rows, 1), f32)
        acc = jnp.zeros((rows, HEAD), f32)
        for j in range(n_kv):
            p = jnp.exp2(scores[j] * EXP_SCALE - new)
            total = total + jnp.sum(p, axis=1, keepdims=True)
            acc = acc + jnp.dot(p.astype(bf16), kv[2 * j + 1][:, at], preferred_element_type=f32)
        old = m_ref[h]
        new = jnp.broadcast_to(new, (rows, HEAD))
        m = jnp.maximum(new, old)
        fade_old, fade_new = jnp.exp2(old - m), jnp.exp2(new - m)
        total = l_ref[h] * fade_old + jnp.broadcast_to(total, (rows, HEAD)) * fade_new
        acc = acc_ref[:, at] * fade_old + acc * fade_new
        attended[:, at] = (acc / total).astype(bf16)
    size = jnp.full((1, TILE), h_ref[0, 1] - h_ref[0, 0], jnp.int32).astype(f32) / 1000.0
    for t in range(TILES):
        at = slice(t * TILE, (t + 1) * TILE)
        proj = jnp.dot(attended[...], w_ref[:, at], preferred_element_type=f32)
        out_ref[:, at] = size * (x_ref[:, at].astype(f32) + gate_ref[:, at] * proj)
    half = sent_ref.shape[0]
    theirs = pl.ds(pl.multiple_of((1 - place_ref[0]) * half, half), half)
    sent_ref[...] = out_ref[theirs, :].astype(bf16)


def finish(step_times, place, q, kvs, state, x, gate, w_out):
    rows = q.shape[0]
    keys = sum(k.shape[0] for k, _ in kvs)
    flat = [a for pair in kvs for a in pair]
    vm = pl.BlockSpec(memory_space=pltpu.VMEM)
    return pl.pallas_call(
        functools.partial(finish_kernel, len(kvs)),
        in_specs=[pl.BlockSpec(memory_space=pltpu.SMEM)] * 2
        + [vm] * (1 + len(flat) + 3 + 3),
        out_specs=[vm] * 2,
        out_shape=[pltpu.VMEM((rows, D), f32), pltpu.VMEM((rows // 2, D), bf16)],
        scratch_shapes=[pltpu.VMEM((rows, D), bf16)],
        cost_estimate=pl.CostEstimate(
            flops=8 * rows * D * keys + 2 * rows * D * D,
            bytes_accessed=2 * D * D,
            transcendentals=rows * keys * HEADS,
        ),
        compiler_params=pltpu.CompilerParams(vmem_limit_bytes=12 << 20),
    )(step_times, place, q, *flat, *state, x, gate, w_out)


def split_kernel(place, inc, got, own, *pieces):
    c, xx = place[0], place[1]
    part = own.shape[0]
    for k, out in enumerate((own,) + pieces):
        at = pl.multiple_of(((xx + k) & 3) * part, part)
        both = inc[pl.ds(pl.multiple_of(c * 4 * part, part) + at, part), :] + got[pl.ds(at, part), :].astype(f32)
        out[...] = both.astype(out.dtype)


def row_kernel(own, one, two, three, out):
    out[...] = (own[...] + one[...].astype(f32) + two[...].astype(f32) + three[...].astype(f32)).astype(bf16)


def before_kernel(place, own, *refs):
    xs, ys, outs = refs[:3], refs[3:6], refs[6:]
    xx, yy = place[1], place[2]
    above = jnp.zeros(own.shape, f32)
    for k in (1, 2, 3):
        above = above + jnp.where(((yy - k) & 3) < yy, ys[k - 1][...].astype(f32), 0.0)
    src = [own[...]] + [r[...].astype(f32) for r in xs]
    for k, out in enumerate(outs):
        total = above
        for j in range(4):
            total = total + jnp.where(((xx - j) & 3) < ((xx + k) & 3), src[j], 0.0)
        out[...] = total.astype(out.dtype)


def join_kernel(place, inc, got, *refs):
    pieces, (own, given) = refs[:4], refs[4:]
    c, xx = place[0], place[1]
    part = pieces[0].shape[0]
    for k in range(4):
        at = pl.multiple_of(((xx - k) & 3) * part, part)
        mine = inc[pl.ds(pl.multiple_of(c * 4 * part, part) + at, part), :]
        theirs = got[pl.ds(at, part), :].astype(f32)
        entering = pieces[k][...].astype(f32)
        even = entering + jnp.where(c == 0, mine, theirs)
        own[pl.ds(at, part), :] = jnp.where(c == 0, even, even + mine)
        given[pl.ds(at, part), :] = jnp.where(c == 0, even, entering).astype(bf16)


def last_kernel(place, inc, own, other, out):
    c, half = place[0], own.shape[0]
    at = pl.multiple_of(c * half, half)
    rest = pl.multiple_of((1 - c) * half, half)
    out[pl.ds(at, half), :] = own[...]
    out[pl.ds(rest, half), :] = other[...].astype(f32) + inc[pl.ds(rest, half), :]


def small_call(kernel, place, args, outs):
    vm = pl.BlockSpec(memory_space=pltpu.VMEM)
    head = [] if place is None else [place]
    return pl.pallas_call(
        kernel,
        in_specs=[pl.BlockSpec(memory_space=pltpu.SMEM)] * len(head) + [vm] * len(args),
        out_specs=[vm] * len(outs),
        out_shape=outs,
        compiler_params=pltpu.CompilerParams(vmem_limit_bytes=3 << 20),
    )(*head, *args)


def scan_steps(place, inc, sent):
    rows = inc.shape[0]
    half, part = rows // 2, rows // 8
    pair = [(i, i ^ 1) for i in range(32)]
    ring = range(4)

    def along_x(k):
        return [((y * 4 + x) * 2 + c, (y * 4 + (x + k) % 4) * 2 + c) for y in ring for x in ring for c in (0, 1)]

    def along_y(k):
        return [((y * 4 + x) * 2 + c, ((y + k) % 4 * 4 + x) * 2 + c) for y in ring for x in ring for c in (0, 1)]

    narrow, wide = pltpu.VMEM((part, D), bf16), pltpu.VMEM((part, D), f32)
    got = lax.ppermute(sent, "step", pair)
    own, *pieces = small_call(split_kernel, place, (inc, got), [wide] + [narrow] * 3)
    xs = [lax.ppermute(piece, "step", along_x(k)) for k, piece in zip((1, 2, 3), pieces)]
    (row,) = small_call(row_kernel, None, (own, *xs), [narrow])
    ys = [lax.ppermute(row, "step", along_y(k)) for k in (1, 2, 3)]
    home, *away = small_call(before_kernel, place, (own, *xs, *ys), [wide] + [narrow] * 3)
    back = [lax.ppermute(piece, "step", along_x(k)) for k, piece in zip((1, 2, 3), away)]
    done, given = small_call(
        join_kernel, place, (inc, got, home, *back), [pltpu.VMEM((half, D), f32), pltpu.VMEM((half, D), bf16)]
    )
    other = lax.ppermute(given, "step", pair)
    return small_call(last_kernel, place, (inc, done, other), [jax.ShapeDtypeStruct((rows, D), f32)])[0]


def on_device(states, step_times, positions, w_qkv, qk_gain, w_out, time_weight):
    n = lax.axis_size("seq")
    right = [(i, (i + 1) % n) for i in range(n)]
    left = [(i, (i - 1) % n) for i in range(n)]
    to_right = lambda v: lax.ppermute(v, "seq", right)
    to_left = lambda v: lax.ppermute(v, "seq", left)
    step = lax.axis_index("step")
    place = jnp.stack([step % 2, (step // 2) % 4, step // 8])

    x = states[0]
    first, second = with_positions(x, positions)
    r_first, l_second = to_right(first), to_left(second)
    ready = (modulation(step_times, time_weight), place, second, first)
    (shift, scale, gate, rates), place, second_later, first_later = lax.optimization_barrier(ready)
    r_second, l_first = to_right(second_later), to_left(first_later)
    forward = to_right(r_first), to_left(l_second)

    q, k, v = project((first_later, second_later), shift, scale, qk_gain, rates, w_qkv, True)
    kvs = [(k, v)]
    for chunk in ((r_first, l_second), (r_second, l_first), forward):
        kvs.append(tuple(project(chunk, shift, scale, qk_gain, rates, w_qkv, False)))
    state = attend(q, kvs[:3])
    inc, sent = finish(step_times, place, q, kvs[3:], state, x, gate, w_out)
    return scan_steps(place, inc, sent)[None]


def solution(mesh):
    placed = (P("step", "seq", None), P("step", None), P("seq"), P(), P(), P(), P())
    return jax.shard_map(
        on_device, mesh=mesh, in_specs=placed, out_specs=P("step", "seq", None), check_vma=False
    )
```

```python
import functools
import math

import jax
import jax.numpy as jnp
from jax import lax
from jax.experimental import pallas as pl
from jax.experimental.pallas import tpu as pltpu
from jax.sharding import PartitionSpec as P

D = 1536
HEAD = 128
HEADS = D // HEAD
TILE = 512
TILES = D // TILE
MESSAGE_VMEM = 63 << 20
HINT = 1 << 33
WIDE = D + HEAD
VMEM = 16 << 20
epsilon = 1e-06
EXP_SCALE = HEAD ** (-0.5) * math.log2(math.e)
f32, bf16 = jnp.float32, jnp.bfloat16


def modulation_kernel(times, weight, first, second, shift, scale, gate, rates, bare_first, bare_second):
    rows, freq = 16, HEAD
    bare_first[...] = first[:, :D]
    bare_second[...] = second[:, :D]
    lane = lax.broadcasted_iota(jnp.int32, (rows, freq), 1)
    row = lax.broadcasted_iota(jnp.int32, (rows, 2 * freq), 0)
    t = jnp.full((rows, freq), times[0, 0], jnp.int32).astype(f32)
    angles = t * jnp.exp(-math.log(10000.0) * lane.astype(f32) / freq)
    embedded = jnp.concatenate([jnp.cos(angles), jnp.sin(angles)], axis=1)
    high = embedded.astype(bf16).astype(f32)
    middle = (embedded - high).astype(bf16).astype(f32)
    low = embedded - high - middle
    terms = jnp.where(row == 0, high, jnp.where(row == 1, middle, jnp.where(row == 2, low, 0.0))).astype(bf16)
    for g, out in enumerate((shift, scale, gate)):
        product = jnp.dot(terms, weight[:, g * D : (g + 1) * D], preferred_element_type=f32)
        out[...] = jnp.sum(product, axis=0, keepdims=True)
    half_width = HEAD // 2
    lane = lax.broadcasted_iota(jnp.int32, (1, HEAD), 1)
    rates[0:1, :] = jnp.exp(-math.log(10000.0) * (lane & (half_width - 1)).astype(f32) / half_width)
    rates[1:2, :] = jnp.where(lane < half_width, -1.0, 1.0)


def modulation(step_times, time_weight, first, second):
    half = first.shape[0]
    vm = pl.BlockSpec(memory_space=pltpu.VMEM)
    return pl.pallas_call(
        modulation_kernel,
        in_specs=[pl.BlockSpec(memory_space=pltpu.SMEM), vm, vm, vm],
        out_specs=[vm] * 6,
        out_shape=[pltpu.VMEM((1, D), f32)] * 3 + [pltpu.VMEM((2, HEAD), f32)] + [pltpu.VMEM((half, D), bf16)] * 2,
        cost_estimate=pl.CostEstimate(flops=HINT, bytes_accessed=0, transcendentals=0),
        compiler_params=pltpu.CompilerParams(vmem_limit_bytes=3 << 20),
    )(step_times, time_weight, first, second)


def message_kernel(x, positions_any, first, second, positions, sems):
    rows = first.shape[0]
    ids_load = pltpu.make_async_copy(positions_any, positions, sems.at[2])
    ids_load.start()
    copies = [
        pltpu.make_async_copy(x.at[pl.ds(j * rows, rows), :], out.at[:, pl.ds(0, D)], sems.at[j])
        for j, out in enumerate((first, second))
    ]
    for copy in copies:
        copy.start()
    lane = lax.broadcasted_iota(jnp.int32, (rows, HEAD), 1)
    row = lax.broadcasted_iota(jnp.int32, (rows, HEAD), 0)
    ids_load.wait()
    digits = []
    for j in range(2):
        spread = jnp.where(row == lane, positions[j : j + 1, :], 0).astype(f32)
        ids = jnp.sum(spread, axis=1, keepdims=True).astype(jnp.int32)
        digits.append((ids >> 5, ids & 31))
    for j, out in enumerate((first, second)):
        mine, others = digits[j], digits[1 - j]
        four = jnp.where(lane == 2, others[0], jnp.where(lane == 3, others[1], 0))
        four = jnp.where(lane == 0, mine[0], jnp.where(lane == 1, mine[1], four))
        out[:, D:] = four.astype(f32).astype(bf16)
    for copy in copies:
        copy.wait()


def with_positions(x, positions):
    half = x.shape[0] // 2
    anywhere = pl.BlockSpec(memory_space=pl.ANY)
    return pl.pallas_call(
        message_kernel,
        in_specs=[anywhere] * 2,
        out_specs=[pl.BlockSpec(memory_space=pltpu.VMEM)] * 2,
        out_shape=[pltpu.VMEM((half, WIDE), bf16)] * 2,
        scratch_shapes=[
            pltpu.VMEM((2, half), jnp.int32),
            pltpu.SemaphoreType.DMA((3,)),
        ],
        cost_estimate=pl.CostEstimate(flops=HINT, bytes_accessed=0, transcendentals=0),
        compiler_params=pltpu.CompilerParams(vmem_limit_bytes=MESSAGE_VMEM),
    )(x, positions.reshape(2, half))


def norm_rope(proj, gain, cos, sin, out_ref):
    rows = proj.shape[0]
    total = jnp.zeros((rows, HEAD), f32)
    for h in range(HEADS):
        p = proj[:, h * HEAD : (h + 1) * HEAD]
        total = total + p * p
    inv = lax.rsqrt(jnp.sum(total, axis=1, keepdims=True) * (1.0 / D) + epsilon)
    for h in range(HEADS):
        at = slice(h * HEAD, (h + 1) * HEAD)
        y = proj[:, at] * inv * gain[:, at]
        out_ref[:, at] = (y * cos + pltpu.roll(y, HEAD // 2, 1) * sin).astype(bf16)


def project_kernel(with_q, n_ids, *refs):
    x_refs, id_refs, (shift, scale, gains, rates, w) = refs[:2], refs[2 : 2 + n_ids], refs[2 + n_ids : 7 + n_ids]
    outs, (normed, proj) = refs[7 + n_ids : -2], refs[-2:]
    at, angles = 0, []
    for x_ref, ids in zip(x_refs, id_refs or x_refs):
        rows = x_ref.shape[0]
        x = x_ref[:, :D].astype(f32)
        inv = lax.rsqrt(jnp.sum(x * x, axis=1, keepdims=True) * (1.0 / D) + epsilon)
        normed[pl.ds(at, rows), :] = (x * inv * (1.0 + scale[...]) + shift[...]).astype(bf16)
        digits = ids[:, D:].astype(f32)
        angles.append((digits[:, n_ids : n_ids + 1] * 32.0 + digits[:, n_ids + 1 : n_ids + 2]) * rates[0:1, :])
        at += rows
    angles = jnp.concatenate(angles, axis=0)
    cos, sin = jnp.cos(angles), jnp.sin(angles) * rates[1:2, :]
    names = ["q", "k", "v"] if with_q else ["k", "v"]
    out_of = dict(zip(names, outs))
    first = {"q": 0, "k": TILES, "v": 2 * TILES}
    for g, name in enumerate(["k", "q", "v"] if with_q else ["k", "v"]):
        for t in range(TILES):
            at = slice(t * TILE, (t + 1) * TILE)
            col = (first[name] + t) * TILE
            acc = jnp.dot(normed[...], w[:, col : col + TILE], preferred_element_type=f32)
            if name == "v":
                out_of[name][:, at] = acc.astype(bf16)
            else:
                proj[g, :, at] = acc
        if name != "v":
            row = 1 if name == "k" else 0
            norm_rope(proj.at[g], gains[row : row + 1, :], cos, sin, out_of[name])


def project(xs, ids, shift, scale, gains, rates, w_qkv, with_q):
    rows = sum(x.shape[0] for x in xs)
    groups = 3 if with_q else 2
    vm = pl.BlockSpec(memory_space=pltpu.VMEM)
    return pl.pallas_call(
        functools.partial(project_kernel, with_q, len(ids)),
        in_specs=[vm] * (7 + len(ids)),
        out_specs=[vm] * groups,
        out_shape=[pltpu.VMEM((rows, D), bf16)] * groups,
        scratch_shapes=[pltpu.VMEM((rows, D), bf16), pltpu.VMEM((groups - 1, rows, D), f32)],
        cost_estimate=pl.CostEstimate(
            flops=2 * rows * D * D * groups, bytes_accessed=2 * D * D * groups, transcendentals=0
        ),
        compiler_params=pltpu.CompilerParams(vmem_limit_bytes=8 << 20),
    )(*xs, *ids, shift, scale, gains, rates, w_qkv)


def merge(new, total, acc, old, old_total, old_acc):
    m = jnp.maximum(new, old)
    fade_old, fade_new = jnp.exp2(old - m), jnp.exp2(new - m)
    return m, old_total * fade_old + total * fade_new, old_acc * fade_old + acc * fade_new


def attend_kernel(n_kv, q_ref, *refs):
    kv, before, (m_ref, l_ref, acc_ref) = refs[: 2 * n_kv], refs[2 * n_kv : -3], refs[-3:]
    rows = q_ref.shape[0]
    for h in range(HEADS):
        at = slice(h * HEAD, (h + 1) * HEAD)
        q = q_ref[:, at]
        scores = [
            lax.dot_general(q, kv[2 * j][:, at], (((1,), (1,)), ((), ())), preferred_element_type=f32)
            for j in range(n_kv)
        ]
        top = scores[0]
        for s in scores[1:]:
            top = jnp.maximum(top, s)
        m = jnp.max(top, axis=1, keepdims=True) * EXP_SCALE
        total = jnp.zeros((rows, 1), f32)
        acc = jnp.zeros((rows, HEAD), f32)
        for j in range(n_kv):
            p = jnp.exp2(scores[j] * EXP_SCALE - m)
            total = total + jnp.sum(p, axis=1, keepdims=True)
            acc = acc + jnp.dot(p.astype(bf16), kv[2 * j + 1][:, at], preferred_element_type=f32)
        m = jnp.broadcast_to(m, (rows, HEAD))
        total = jnp.broadcast_to(total, (rows, HEAD))
        if before:
            m, total, acc = merge(m, total, acc, before[0][h], before[1][h], before[2][:, at])
        m_ref[h] = m
        l_ref[h] = total
        acc_ref[:, at] = acc


def attend(q, kvs, before=()):
    rows = q.shape[0]
    keys = sum(k.shape[0] for k, _ in kvs)
    flat = [a for pair in kvs for a in pair]
    vm = pl.BlockSpec(memory_space=pltpu.VMEM)
    return pl.pallas_call(
        functools.partial(attend_kernel, len(kvs)),
        in_specs=[vm] * (1 + len(flat) + len(before)),
        out_specs=[vm] * 3,
        out_shape=[
            pltpu.VMEM((HEADS, rows, HEAD), f32),
            pltpu.VMEM((HEADS, rows, HEAD), f32),
            pltpu.VMEM((rows, D), f32),
        ],
        cost_estimate=pl.CostEstimate(
            flops=8 * rows * D * keys, bytes_accessed=4 * rows * D * 2, transcendentals=rows * keys * HEADS
        ),
        compiler_params=pltpu.CompilerParams(vmem_limit_bytes=12 << 20),
    )(q, *flat, *before)


def finish_kernel(theirs, times, place, q_ref, k_ref, v_ref, m_ref, l_ref, acc_ref, x_ref, gate_ref, w_ref, *refs):
    out_ref, attended = refs[0], refs[-1]
    half = out_ref.shape[0]
    which = 1 - place[0] if theirs else place[0]
    rows = pl.ds(pl.multiple_of(which * half, half), half)
    for h in range(HEADS):
        at = slice(h * HEAD, (h + 1) * HEAD)
        s = lax.dot_general(
            q_ref[rows, at], k_ref[:, at], (((1,), (1,)), ((), ())), preferred_element_type=f32
        )
        new = jnp.max(s, axis=1, keepdims=True) * EXP_SCALE
        p = jnp.exp2(s * EXP_SCALE - new)
        total = jnp.broadcast_to(jnp.sum(p, axis=1, keepdims=True), (half, HEAD))
        acc = jnp.dot(p.astype(bf16), v_ref[:, at], preferred_element_type=f32)
        new = jnp.broadcast_to(new, (half, HEAD))
        _, total, acc = merge(new, total, acc, m_ref[h, rows, :], l_ref[h, rows, :], acc_ref[rows, at])
        attended[:, at] = (acc / total).astype(bf16)
    size = jnp.full((1, TILE), times[0, 1] - times[0, 0], jnp.int32).astype(f32) / 1000.0
    for t in range(TILES):
        at = slice(t * TILE, (t + 1) * TILE)
        proj = jnp.dot(attended[...], w_ref[:, at], preferred_element_type=f32)
        inc = size * (x_ref[rows, at].astype(f32) + gate_ref[:, at] * proj)
        out_ref[:, at] = inc
        if theirs:
            refs[1][:, at] = inc.astype(bf16)


def finish(theirs, step_times, place, q, kv, state, x, gate, w_out):
    half = q.shape[0] // 2
    keys = kv[0].shape[0]
    vm = pl.BlockSpec(memory_space=pltpu.VMEM)
    outs = [pltpu.VMEM((half, D), f32)] + [pltpu.VMEM((half, D), bf16)] * theirs
    return pl.pallas_call(
        functools.partial(finish_kernel, theirs),
        in_specs=[pl.BlockSpec(memory_space=pltpu.SMEM)] * 2 + [vm] * 9,
        out_specs=[vm] * len(outs),
        out_shape=outs,
        scratch_shapes=[pltpu.VMEM((half, D), bf16)],
        cost_estimate=pl.CostEstimate(
            flops=8 * half * D * keys + 2 * half * D * D,
            bytes_accessed=2 * D * D,
            transcendentals=half * keys * HEADS,
        ),
        compiler_params=pltpu.CompilerParams(vmem_limit_bytes=12 << 20),
    )(step_times, place, q, *kv, *state, x, gate, w_out)


def split_kernel(place, mine, got, own, *pieces):
    xx = place[1]
    part = own.shape[0]
    for k, out in enumerate((own,) + pieces):
        at = pl.multiple_of(((xx + k) & 3) * part, part)
        both = mine[pl.ds(at, part), :] + got[pl.ds(at, part), :].astype(f32)
        out[...] = both.astype(out.dtype)


def row_kernel(own, one, two, three, out):
    out[...] = (own[...] + one[...].astype(f32) + two[...].astype(f32) + three[...].astype(f32)).astype(bf16)


def before_kernel(place, own, *refs):
    xs, ys, outs = refs[:3], refs[3:6], refs[6:]
    xx, yy = place[1], place[2]
    above = jnp.zeros(own.shape, f32)
    for k in (1, 2, 3):
        above = above + jnp.where(((yy - k) & 3) < yy, ys[k - 1][...].astype(f32), 0.0)
    src = [own[...]] + [r[...].astype(f32) for r in xs]
    for k, out in enumerate(outs):
        total = above
        for j in range(4):
            total = total + jnp.where(((xx - j) & 3) < ((xx + k) & 3), src[j], 0.0)
        out[...] = total.astype(out.dtype)


def given_kernel(place, mine, *refs):
    pieces, given = refs[:4], refs[4]
    c, xx = place[0], place[1]
    part = pieces[0].shape[0]
    for k in range(4):
        at = pl.ds(pl.multiple_of(((xx - k) & 3) * part, part), part)
        given[at, :] = (pieces[k][...].astype(f32) + jnp.where(c == 0, mine[at, :], 0.0)).astype(bf16)


def own_half_kernel(place, mine, got, *refs):
    pieces, (out, held, sem) = refs[:4], refs[4:]
    c, xx = place[0], place[1]
    part, half = pieces[0].shape[0], held.shape[0]
    for k in range(4):
        at = pl.ds(pl.multiple_of(((xx - k) & 3) * part, part), part)
        held[at, :] = pieces[k][...].astype(f32) + mine[at, :] + jnp.where(c == 0, 0.0, got[at, :].astype(f32))
    store = pltpu.make_async_copy(held, out.at[pl.ds(pl.multiple_of(c * half, half), half), :], sem)
    store.start()
    store.wait()


def other_half_kernel(place, theirs, other, begun, out, held, sem):
    half = held.shape[0]
    held[...] = other[...].astype(f32) + theirs[...]
    at = pl.multiple_of((1 - place[0]) * half, half)
    store = pltpu.make_async_copy(held, out.at[pl.ds(at, half), :], sem)
    store.start()
    store.wait()


def store_call(kernel, place, args, begun, rows):
    vm, anywhere = pl.BlockSpec(memory_space=pltpu.VMEM), pl.BlockSpec(memory_space=pl.ANY)
    return pl.pallas_call(
        kernel,
        in_specs=[pl.BlockSpec(memory_space=pltpu.SMEM)] + [vm] * len(args) + [anywhere] * len(begun),
        out_specs=anywhere,
        out_shape=jax.ShapeDtypeStruct((rows, D), f32),
        scratch_shapes=[pltpu.VMEM((rows // 2, D), f32), pltpu.SemaphoreType.DMA],
        input_output_aliases={1 + len(args): 0} if begun else {},
        cost_estimate=pl.CostEstimate(flops=0, bytes_accessed=6 * rows * D, transcendentals=0),
        compiler_params=pltpu.CompilerParams(vmem_limit_bytes=4 << 20),
    )(place, *args, *begun)


def small_call(kernel, place, args, outs):
    vm = pl.BlockSpec(memory_space=pltpu.VMEM)
    head = [] if place is None else [place]
    return pl.pallas_call(
        kernel,
        in_specs=[pl.BlockSpec(memory_space=pltpu.SMEM)] * len(head) + [vm] * len(args),
        out_specs=[vm] * len(outs),
        out_shape=outs,
        compiler_params=pltpu.CompilerParams(vmem_limit_bytes=3 << 20),
    )(*head, *args)


def scan_steps(place, mine, theirs, sent):
    half = mine.shape[0]
    part = half // 4
    pair = [(i, i ^ 1) for i in range(32)]
    ring = range(4)

    def along_x(k):
        return [((y * 4 + x) * 2 + c, (y * 4 + (x + k) % 4) * 2 + c) for y in ring for x in ring for c in (0, 1)]

    def along_y(k):
        return [((y * 4 + x) * 2 + c, ((y + k) % 4 * 4 + x) * 2 + c) for y in ring for x in ring for c in (0, 1)]

    narrow, wide = pltpu.VMEM((part, D), bf16), pltpu.VMEM((part, D), f32)
    got = lax.ppermute(sent, "step", pair)
    own, *pieces = small_call(split_kernel, place, (mine, got), [wide] + [narrow] * 3)
    xs = [lax.ppermute(piece, "step", along_x(k)) for k, piece in zip((1, 2, 3), pieces)]
    (row,) = small_call(row_kernel, None, (own, *xs), [narrow])
    ys = [lax.ppermute(row, "step", along_y(k)) for k in (1, 2, 3)]
    home, *away = small_call(before_kernel, place, (own, *xs, *ys), [wide] + [narrow] * 3)
    back = [lax.ppermute(piece, "step", along_x(k)) for k, piece in zip((1, 2, 3), away)]
    (given,) = small_call(given_kernel, place, (mine, home, *back), [pltpu.VMEM((half, D), bf16)])
    other = lax.ppermute(given, "step", pair)
    begun = store_call(own_half_kernel, place, (mine, got, home, *back), (), 2 * half)
    return store_call(other_half_kernel, place, (theirs, other), (begun,), 2 * half)


def on_device(states, step_times, positions, w_qkv, qk_gain, w_out, time_weight):
    n = lax.axis_size("seq")
    right = [(i, (i + 1) % n) for i in range(n)]
    left = [(i, (i - 1) % n) for i in range(n)]
    to_right = lambda v: lax.ppermute(v, "seq", right)
    to_left = lambda v: lax.ppermute(v, "seq", left)
    step = lax.axis_index("step")
    place = jnp.stack([step % 2, (step // 2) % 4, step // 8])

    x = states[0]
    first, second = with_positions(x, positions)
    r_first, l_second = to_right(first), to_left(second)
    modulated = modulation(step_times, time_weight, first, second)
    shift, scale, gate, rates, bare_first, bare_second, place = lax.optimization_barrier((*modulated, place))
    r_second, l_first = to_right(bare_second), to_left(bare_first)
    forward = to_right(r_first), to_left(l_second)

    given = (shift, scale, qk_gain, rates, w_qkv)
    q, k, v = project((first, second), (), *given, True)
    near = project((r_first, l_second), (), *given, False)
    next_near = project((r_second, l_first), (r_first, l_second), *given, False)
    far = project(forward, (), *given, False)
    state = attend(q, [next_near], attend(q, [(k, v), near]))
    late = (step_times, place, q, far, state, x, gate, w_out)
    theirs, sent = finish(True, *late)
    (mine,) = finish(False, *late)
    return scan_steps(place, mine, theirs, sent)[None]


def solution(mesh):
    placed = (P("step", "seq", None), P("step", None), P("seq"), P(), P(), P(), P())
    return jax.shard_map(
        on_device, mesh=mesh, in_specs=placed, out_specs=P("step", "seq", None), check_vma=False
    )
```

```python
import functools
import math

import jax
import jax.numpy as jnp
from jax import lax
from jax.experimental import pallas as pl
from jax.experimental.pallas import tpu as pltpu
from jax.sharding import PartitionSpec as P

D = 1536
HEAD = 128
HEADS = D // HEAD
TILE = 512
TILES = D // TILE
MESSAGE_VMEM = 63 << 20
HINT = 1 << 33
WIDE = D + HEAD
VMEM = 16 << 20
epsilon = 1e-06
EXP_SCALE = HEAD ** (-0.5) * math.log2(math.e)
f32, bf16 = jnp.float32, jnp.bfloat16


def modulation_kernel(times, weight, first, second, shift, scale, gate, rates, bare_first, bare_second):
    rows, freq = 16, HEAD
    bare_first[...] = first[:, :D]
    bare_second[...] = second[:, :D]
    lane = lax.broadcasted_iota(jnp.int32, (rows, freq), 1)
    row = lax.broadcasted_iota(jnp.int32, (rows, 2 * freq), 0)
    t = jnp.full((rows, freq), times[0, 0], jnp.int32).astype(f32)
    angles = t * jnp.exp(-math.log(10000.0) * lane.astype(f32) / freq)
    embedded = jnp.concatenate([jnp.cos(angles), jnp.sin(angles)], axis=1)
    high = embedded.astype(bf16).astype(f32)
    middle = (embedded - high).astype(bf16).astype(f32)
    low = embedded - high - middle
    terms = jnp.where(row == 0, high, jnp.where(row == 1, middle, jnp.where(row == 2, low, 0.0))).astype(bf16)
    for g, out in enumerate((shift, scale, gate)):
        product = jnp.dot(terms, weight[:, g * D : (g + 1) * D], preferred_element_type=f32)
        out[...] = jnp.sum(product, axis=0, keepdims=True)
    half_width = HEAD // 2
    lane = lax.broadcasted_iota(jnp.int32, (1, HEAD), 1)
    rates[0:1, :] = jnp.exp(-math.log(10000.0) * (lane & (half_width - 1)).astype(f32) / half_width)
    rates[1:2, :] = jnp.where(lane < half_width, -1.0, 1.0)


def modulation(step_times, time_weight, first, second):
    half = first.shape[0]
    vm = pl.BlockSpec(memory_space=pltpu.VMEM)
    return pl.pallas_call(
        modulation_kernel,
        in_specs=[pl.BlockSpec(memory_space=pltpu.SMEM), vm, vm, vm],
        out_specs=[vm] * 6,
        out_shape=[pltpu.VMEM((1, D), f32)] * 3 + [pltpu.VMEM((2, HEAD), f32)] + [pltpu.VMEM((half, D), bf16)] * 2,
        cost_estimate=pl.CostEstimate(flops=HINT, bytes_accessed=0, transcendentals=0),
        compiler_params=pltpu.CompilerParams(vmem_limit_bytes=3 << 20),
    )(step_times, time_weight, first, second)


def message_kernel(x, positions_any, first, second, positions, sems):
    rows = first.shape[0]
    ids_load = pltpu.make_async_copy(positions_any, positions, sems.at[2])
    ids_load.start()
    copies = [
        pltpu.make_async_copy(x.at[pl.ds(j * rows, rows), :], out.at[:, pl.ds(0, D)], sems.at[j])
        for j, out in enumerate((first, second))
    ]
    for copy in copies:
        copy.start()
    lane = lax.broadcasted_iota(jnp.int32, (rows, HEAD), 1)
    row = lax.broadcasted_iota(jnp.int32, (rows, HEAD), 0)
    ids_load.wait()
    digits = []
    for j in range(2):
        spread = jnp.where(row == lane, positions[j : j + 1, :], 0).astype(f32)
        ids = jnp.sum(spread, axis=1, keepdims=True).astype(jnp.int32)
        digits.append((ids >> 5, ids & 31))
    for j, out in enumerate((first, second)):
        mine, others = digits[j], digits[1 - j]
        four = jnp.where(lane == 2, others[0], jnp.where(lane == 3, others[1], 0))
        four = jnp.where(lane == 0, mine[0], jnp.where(lane == 1, mine[1], four))
        out[:, D:] = four.astype(f32).astype(bf16)
    for copy in copies:
        copy.wait()


def with_positions(x, positions):
    half = x.shape[0] // 2
    anywhere = pl.BlockSpec(memory_space=pl.ANY)
    return pl.pallas_call(
        message_kernel,
        in_specs=[anywhere] * 2,
        out_specs=[pl.BlockSpec(memory_space=pltpu.VMEM)] * 2,
        out_shape=[pltpu.VMEM((half, WIDE), bf16)] * 2,
        scratch_shapes=[
            pltpu.VMEM((2, half), jnp.int32),
            pltpu.SemaphoreType.DMA((3,)),
        ],
        cost_estimate=pl.CostEstimate(flops=HINT, bytes_accessed=0, transcendentals=0),
        compiler_params=pltpu.CompilerParams(vmem_limit_bytes=MESSAGE_VMEM),
    )(x, positions.reshape(2, half))


def norm_rope(proj, gain, cos, sin, out_ref):
    rows = proj.shape[0]
    total = jnp.zeros((rows, HEAD), f32)
    for h in range(HEADS):
        p = proj[:, h * HEAD : (h + 1) * HEAD]
        total = total + p * p
    inv = lax.rsqrt(jnp.sum(total, axis=1, keepdims=True) * (1.0 / D) + epsilon)
    for h in range(HEADS):
        at = slice(h * HEAD, (h + 1) * HEAD)
        y = proj[:, at] * inv * gain[:, at]
        out_ref[:, at] = (y * cos + pltpu.roll(y, HEAD // 2, 1) * sin).astype(bf16)


def project_kernel(with_q, n_ids, *refs):
    x_refs, id_refs, (shift, scale, gains, rates, w) = refs[:2], refs[2 : 2 + n_ids], refs[2 + n_ids : 7 + n_ids]
    outs, (normed, proj) = refs[7 + n_ids : -2], refs[-2:]
    at, angles = 0, []
    for x_ref, ids in zip(x_refs, id_refs or x_refs):
        rows = x_ref.shape[0]
        x = x_ref[:, :D].astype(f32)
        inv = lax.rsqrt(jnp.sum(x * x, axis=1, keepdims=True) * (1.0 / D) + epsilon)
        normed[pl.ds(at, rows), :] = (x * inv * (1.0 + scale[...]) + shift[...]).astype(bf16)
        digits = ids[:, D:].astype(f32)
        angles.append((digits[:, n_ids : n_ids + 1] * 32.0 + digits[:, n_ids + 1 : n_ids + 2]) * rates[0:1, :])
        at += rows
    angles = jnp.concatenate(angles, axis=0)
    cos, sin = jnp.cos(angles), jnp.sin(angles) * rates[1:2, :]
    names = ["q", "k", "v"] if with_q else ["k", "v"]
    out_of = dict(zip(names, outs))
    first = {"q": 0, "k": TILES, "v": 2 * TILES}
    for g, name in enumerate(["k", "q", "v"] if with_q else ["k", "v"]):
        for t in range(TILES):
            at = slice(t * TILE, (t + 1) * TILE)
            col = (first[name] + t) * TILE
            acc = jnp.dot(normed[...], w[:, col : col + TILE], preferred_element_type=f32)
            if name == "v":
                out_of[name][:, at] = acc.astype(bf16)
            else:
                proj[g, :, at] = acc
        if name != "v":
            row = 1 if name == "k" else 0
            norm_rope(proj.at[g], gains[row : row + 1, :], cos, sin, out_of[name])


def project(xs, ids, shift, scale, gains, rates, w_qkv, with_q):
    rows = sum(x.shape[0] for x in xs)
    groups = 3 if with_q else 2
    vm = pl.BlockSpec(memory_space=pltpu.VMEM)
    return pl.pallas_call(
        functools.partial(project_kernel, with_q, len(ids)),
        in_specs=[vm] * (7 + len(ids)),
        out_specs=[vm] * groups,
        out_shape=[pltpu.VMEM((rows, D), bf16)] * groups,
        scratch_shapes=[pltpu.VMEM((rows, D), bf16), pltpu.VMEM((groups - 1, rows, D), f32)],
        cost_estimate=pl.CostEstimate(
            flops=2 * rows * D * D * groups, bytes_accessed=2 * D * D * groups, transcendentals=0
        ),
        compiler_params=pltpu.CompilerParams(vmem_limit_bytes=8 << 20),
    )(*xs, *ids, shift, scale, gains, rates, w_qkv)


def merge(new, total, acc, old, old_total, old_acc):
    m = jnp.maximum(new, old)
    fade_old, fade_new = jnp.exp2(old - m), jnp.exp2(new - m)
    return m, old_total * fade_old + total * fade_new, old_acc * fade_old + acc * fade_new


def attend_kernel(n_kv, q_ref, *refs):
    kv, before, (m_ref, l_ref, acc_ref) = refs[: 2 * n_kv], refs[2 * n_kv : -3], refs[-3:]
    rows = q_ref.shape[0]
    for h in range(HEADS):
        at = slice(h * HEAD, (h + 1) * HEAD)
        q = q_ref[:, at]
        scores = [
            lax.dot_general(q, kv[2 * j][:, at], (((1,), (1,)), ((), ())), preferred_element_type=f32)
            for j in range(n_kv)
        ]
        top = scores[0]
        for s in scores[1:]:
            top = jnp.maximum(top, s)
        m = jnp.max(top, axis=1, keepdims=True) * EXP_SCALE
        total = jnp.zeros((rows, 1), f32)
        acc = jnp.zeros((rows, HEAD), f32)
        for j in range(n_kv):
            p = jnp.exp2(scores[j] * EXP_SCALE - m)
            total = total + jnp.sum(p, axis=1, keepdims=True)
            acc = acc + jnp.dot(p.astype(bf16), kv[2 * j + 1][:, at], preferred_element_type=f32)
        m = jnp.broadcast_to(m, (rows, HEAD))
        total = jnp.broadcast_to(total, (rows, HEAD))
        if before:
            m, total, acc = merge(m, total, acc, before[0][h], before[1][h], before[2][:, at])
        m_ref[h] = m
        l_ref[h] = total
        acc_ref[:, at] = acc


def attend(q, kvs, before=()):
    rows = q.shape[0]
    keys = sum(k.shape[0] for k, _ in kvs)
    flat = [a for pair in kvs for a in pair]
    vm = pl.BlockSpec(memory_space=pltpu.VMEM)
    return pl.pallas_call(
        functools.partial(attend_kernel, len(kvs)),
        in_specs=[vm] * (1 + len(flat) + len(before)),
        out_specs=[vm] * 3,
        out_shape=[
            pltpu.VMEM((HEADS, rows, HEAD), f32),
            pltpu.VMEM((HEADS, rows, HEAD), f32),
            pltpu.VMEM((rows, D), f32),
        ],
        cost_estimate=pl.CostEstimate(
            flops=8 * rows * D * keys, bytes_accessed=4 * rows * D * 2, transcendentals=rows * keys * HEADS
        ),
        compiler_params=pltpu.CompilerParams(vmem_limit_bytes=12 << 20),
    )(q, *flat, *before)


def finish_kernel(theirs, times, place, q_ref, k_ref, v_ref, m_ref, l_ref, acc_ref, x_ref, gate_ref, w_ref, *refs):
    out_ref, attended = refs[0], refs[-1]
    half = out_ref.shape[0]
    which = 1 - place[0] if theirs else place[0]
    rows = pl.ds(pl.multiple_of(which * half, half), half)
    for h in range(HEADS):
        at = slice(h * HEAD, (h + 1) * HEAD)
        s = lax.dot_general(
            q_ref[rows, at], k_ref[:, at], (((1,), (1,)), ((), ())), preferred_element_type=f32
        )
        new = jnp.max(s, axis=1, keepdims=True) * EXP_SCALE
        p = jnp.exp2(s * EXP_SCALE - new)
        total = jnp.broadcast_to(jnp.sum(p, axis=1, keepdims=True), (half, HEAD))
        acc = jnp.dot(p.astype(bf16), v_ref[:, at], preferred_element_type=f32)
        new = jnp.broadcast_to(new, (half, HEAD))
        _, total, acc = merge(new, total, acc, m_ref[h, rows, :], l_ref[h, rows, :], acc_ref[rows, at])
        attended[:, at] = (acc / total).astype(bf16)
    size = jnp.full((1, TILE), times[0, 1] - times[0, 0], jnp.int32).astype(f32) / 1000.0
    for t in range(TILES):
        at = slice(t * TILE, (t + 1) * TILE)
        proj = jnp.dot(attended[...], w_ref[:, at], preferred_element_type=f32)
        inc = size * (x_ref[rows, at].astype(f32) + gate_ref[:, at] * proj)
        out_ref[:, at] = inc
        if theirs:
            refs[1][:, at] = inc.astype(bf16)


def finish(theirs, step_times, place, q, kv, state, x, gate, w_out):
    half = q.shape[0] // 2
    keys = kv[0].shape[0]
    vm = pl.BlockSpec(memory_space=pltpu.VMEM)
    outs = [pltpu.VMEM((half, D), f32)] + [pltpu.VMEM((half, D), bf16)] * theirs
    return pl.pallas_call(
        functools.partial(finish_kernel, theirs),
        in_specs=[pl.BlockSpec(memory_space=pltpu.SMEM)] * 2 + [vm] * 9,
        out_specs=[vm] * len(outs),
        out_shape=outs,
        scratch_shapes=[pltpu.VMEM((half, D), bf16)],
        cost_estimate=pl.CostEstimate(
            flops=8 * half * D * keys + 2 * half * D * D,
            bytes_accessed=2 * D * D,
            transcendentals=half * keys * HEADS,
        ),
        compiler_params=pltpu.CompilerParams(vmem_limit_bytes=12 << 20),
    )(step_times, place, q, *kv, *state, x, gate, w_out)


def for_each_column(place, body):
    for xx in range(4):
        pl.when(place[1] == xx)(functools.partial(body, xx))


def split_kernel(place, mine, got, own, *pieces):
    part = own.shape[0]

    def split(xx):
        for k, out in enumerate((own,) + pieces):
            at = pl.ds((xx + k) % 4 * part, part)
            out[...] = (mine[at, :] + got[at, :].astype(f32)).astype(out.dtype)

    for_each_column(place, split)


def row_kernel(own, one, two, three, out):
    out[...] = (own[...] + one[...].astype(f32) + two[...].astype(f32) + three[...].astype(f32)).astype(bf16)


def before_kernel(place, own, *refs):
    xs, ys, outs = refs[:3], refs[3:6], refs[6:]
    yy = place[2]
    outs[0][...] = jnp.zeros(own.shape, f32)
    for k in (1, 2, 3):

        @pl.when(((yy - k) & 3) < yy)
        def _(k=k):
            outs[0][...] += ys[k - 1][...].astype(f32)

    def prefix(xx):
        total = outs[0][...]
        for chip in range(4):
            outs[(chip - xx) % 4][...] = total.astype(outs[(chip - xx) % 4].dtype)
            if chip < 3:
                j = (xx - chip) % 4
                total = total + (own if j == 0 else xs[j - 1])[...].astype(f32)

    for_each_column(place, prefix)


def given_kernel(place, mine, *refs):
    pieces, given = refs[:4], refs[4]
    part = pieces[0].shape[0]

    def join(xx):
        for k in range(4):
            at = pl.ds((xx - k) % 4 * part, part)
            given[at, :] = (pieces[k][...].astype(f32) + jnp.where(place[0] == 0, mine[at, :], 0.0)).astype(bf16)

    for_each_column(place, join)


def own_half_kernel(place, mine, got, *refs):
    pieces, (out, held, sem) = refs[:4], refs[4:]
    c, xx = place[0], place[1]
    part, half = pieces[0].shape[0], held.shape[0]
    for k in range(4):
        at = pl.ds(pl.multiple_of(((xx - k) & 3) * part, part), part)
        held[at, :] = pieces[k][...].astype(f32) + mine[at, :] + jnp.where(c == 0, 0.0, got[at, :].astype(f32))
    store = pltpu.make_async_copy(held, out.at[pl.ds(pl.multiple_of(c * half, half), half), :], sem)
    store.start()
    store.wait()


def other_half_kernel(place, theirs, other, begun, out, held, sem):
    half = held.shape[0]
    held[...] = other[...].astype(f32) + theirs[...]
    at = pl.multiple_of((1 - place[0]) * half, half)
    store = pltpu.make_async_copy(held, out.at[pl.ds(at, half), :], sem)
    store.start()
    store.wait()


def store_call(kernel, place, args, begun, rows):
    vm, anywhere = pl.BlockSpec(memory_space=pltpu.VMEM), pl.BlockSpec(memory_space=pl.ANY)
    return pl.pallas_call(
        kernel,
        in_specs=[pl.BlockSpec(memory_space=pltpu.SMEM)] + [vm] * len(args) + [anywhere] * len(begun),
        out_specs=anywhere,
        out_shape=jax.ShapeDtypeStruct((rows, D), f32),
        scratch_shapes=[pltpu.VMEM((rows // 2, D), f32), pltpu.SemaphoreType.DMA],
        input_output_aliases={1 + len(args): 0} if begun else {},
        cost_estimate=pl.CostEstimate(flops=0, bytes_accessed=6 * rows * D, transcendentals=0),
        compiler_params=pltpu.CompilerParams(vmem_limit_bytes=4 << 20),
    )(place, *args, *begun)


def small_call(kernel, place, args, outs):
    vm = pl.BlockSpec(memory_space=pltpu.VMEM)
    head = [] if place is None else [place]
    return pl.pallas_call(
        kernel,
        in_specs=[pl.BlockSpec(memory_space=pltpu.SMEM)] * len(head) + [vm] * len(args),
        out_specs=[vm] * len(outs),
        out_shape=outs,
        compiler_params=pltpu.CompilerParams(vmem_limit_bytes=3 << 20),
    )(*head, *args)


def scan_steps(place, mine, theirs, sent):
    half = mine.shape[0]
    part = half // 4
    pair = [(i, i ^ 1) for i in range(32)]
    ring = range(4)

    def along_x(k):
        return [((y * 4 + x) * 2 + c, (y * 4 + (x + k) % 4) * 2 + c) for y in ring for x in ring for c in (0, 1)]

    def along_y(k):
        return [((y * 4 + x) * 2 + c, ((y + k) % 4 * 4 + x) * 2 + c) for y in ring for x in ring for c in (0, 1)]

    narrow, wide = pltpu.VMEM((part, D), bf16), pltpu.VMEM((part, D), f32)
    got = lax.ppermute(sent, "step", pair)
    own, *pieces = small_call(split_kernel, place, (mine, got), [wide] + [narrow] * 3)
    xs = [lax.ppermute(piece, "step", along_x(k)) for k, piece in zip((1, 2, 3), pieces)]
    (row,) = small_call(row_kernel, None, (own, *xs), [narrow])
    ys = [lax.ppermute(row, "step", along_y(k)) for k in (1, 2, 3)]
    home, *away = small_call(before_kernel, place, (own, *xs, *ys), [wide] + [narrow] * 3)
    back = [lax.ppermute(piece, "step", along_x(k)) for k, piece in zip((1, 2, 3), away)]
    (given,) = small_call(given_kernel, place, (mine, home, *back), [pltpu.VMEM((half, D), bf16)])
    other = lax.ppermute(given, "step", pair)
    begun = store_call(own_half_kernel, place, (mine, got, home, *back), (), 2 * half)
    return store_call(other_half_kernel, place, (theirs, other), (begun,), 2 * half)


def on_device(states, step_times, positions, w_qkv, qk_gain, w_out, time_weight):
    n = lax.axis_size("seq")
    right = [(i, (i + 1) % n) for i in range(n)]
    left = [(i, (i - 1) % n) for i in range(n)]
    to_right = lambda v: lax.ppermute(v, "seq", right)
    to_left = lambda v: lax.ppermute(v, "seq", left)
    step = lax.axis_index("step")
    place = jnp.stack([step % 2, (step // 2) % 4, step // 8])

    x = states[0]
    first, second = with_positions(x, positions)
    r_first, l_second = to_right(first), to_left(second)
    modulated = modulation(step_times, time_weight, first, second)
    shift, scale, gate, rates, bare_first, bare_second, place = lax.optimization_barrier((*modulated, place))
    r_second, l_first = to_right(bare_second), to_left(bare_first)
    forward = to_right(r_first), to_left(l_second)

    given = (shift, scale, qk_gain, rates, w_qkv)
    q, k, v = project((first, second), (), *given, True)
    near = project((r_first, l_second), (), *given, False)
    next_near = project((r_second, l_first), (r_first, l_second), *given, False)
    far = project(forward, (), *given, False)
    state = attend(q, [next_near], attend(q, [(k, v), near]))
    late = (step_times, place, q, far, state, x, gate, w_out)
    theirs, sent = finish(True, *late)
    (mine,) = finish(False, *late)
    return scan_steps(place, mine, theirs, sent)[None]


def solution(mesh):
    placed = (P("step", "seq", None), P("step", None), P("seq"), P(), P(), P(), P())
    return jax.shard_map(
        on_device, mesh=mesh, in_specs=placed, out_specs=P("step", "seq", None), check_vma=False
    )
```

```python
import functools
import math

import jax
import jax.numpy as jnp
from jax import lax
from jax.experimental import pallas as pl
from jax.experimental.pallas import tpu as pltpu
from jax.sharding import PartitionSpec as P

D = 1536
HEAD = 128
HEADS = D // HEAD
TILE = 512
TILES = D // TILE
MESSAGE_VMEM = 63 << 20
HINT = 1 << 33
WIDE = D + HEAD
VMEM = 16 << 20
epsilon = 1e-06
EXP_SCALE = HEAD ** (-0.5) * math.log2(math.e)
f32, bf16 = jnp.float32, jnp.bfloat16


def modulation_kernel(times, weight, first, second, shift, scale, gate, rates, bare_first, bare_second):
    rows, freq = 16, HEAD
    bare_first[...] = first[:, :D]
    bare_second[...] = second[:, :D]
    lane = lax.broadcasted_iota(jnp.int32, (rows, freq), 1)
    row = lax.broadcasted_iota(jnp.int32, (rows, 2 * freq), 0)
    t = jnp.full((rows, freq), times[0, 0], jnp.int32).astype(f32)
    angles = t * jnp.exp(-math.log(10000.0) * lane.astype(f32) / freq)
    embedded = jnp.concatenate([jnp.cos(angles), jnp.sin(angles)], axis=1)
    high = embedded.astype(bf16).astype(f32)
    middle = (embedded - high).astype(bf16).astype(f32)
    low = embedded - high - middle
    terms = jnp.where(row == 0, high, jnp.where(row == 1, middle, jnp.where(row == 2, low, 0.0))).astype(bf16)
    for g, out in enumerate((shift, scale, gate)):
        product = jnp.dot(terms, weight[:, g * D : (g + 1) * D], preferred_element_type=f32)
        out[...] = jnp.sum(product, axis=0, keepdims=True)
    half_width = HEAD // 2
    lane = lax.broadcasted_iota(jnp.int32, (1, HEAD), 1)
    rates[0:1, :] = jnp.exp(-math.log(10000.0) * (lane & (half_width - 1)).astype(f32) / half_width)
    rates[1:2, :] = jnp.where(lane < half_width, -1.0, 1.0)


def modulation(step_times, time_weight, first, second):
    half = first.shape[0]
    vm = pl.BlockSpec(memory_space=pltpu.VMEM)
    return pl.pallas_call(
        modulation_kernel,
        in_specs=[pl.BlockSpec(memory_space=pltpu.SMEM), vm, vm, vm],
        out_specs=[vm] * 6,
        out_shape=[pltpu.VMEM((1, D), f32)] * 3 + [pltpu.VMEM((2, HEAD), f32)] + [pltpu.VMEM((half, D), bf16)] * 2,
        cost_estimate=pl.CostEstimate(flops=HINT, bytes_accessed=0, transcendentals=0),
        compiler_params=pltpu.CompilerParams(vmem_limit_bytes=3 << 20),
    )(step_times, time_weight, first, second)


def message_kernel(x, positions_any, first, second, positions, sems):
    rows = first.shape[0]
    ids_load = pltpu.make_async_copy(positions_any, positions, sems.at[2])
    ids_load.start()
    copies = [
        pltpu.make_async_copy(x.at[pl.ds(j * rows, rows), :], out.at[:, pl.ds(0, D)], sems.at[j])
        for j, out in enumerate((first, second))
    ]
    for copy in copies:
        copy.start()
    lane = lax.broadcasted_iota(jnp.int32, (rows, HEAD), 1)
    row = lax.broadcasted_iota(jnp.int32, (rows, HEAD), 0)
    ids_load.wait()
    digits = []
    for j in range(2):
        spread = jnp.where(row == lane, positions[j : j + 1, :], 0).astype(f32)
        ids = jnp.sum(spread, axis=1, keepdims=True).astype(jnp.int32)
        digits.append((ids >> 5, ids & 31))
    for j, out in enumerate((first, second)):
        mine, others = digits[j], digits[1 - j]
        four = jnp.where(lane == 2, others[0], jnp.where(lane == 3, others[1], 0))
        four = jnp.where(lane == 0, mine[0], jnp.where(lane == 1, mine[1], four))
        out[:, D:] = four.astype(f32).astype(bf16)
    for copy in copies:
        copy.wait()


def with_positions(x, positions):
    half = x.shape[0] // 2
    anywhere = pl.BlockSpec(memory_space=pl.ANY)
    return pl.pallas_call(
        message_kernel,
        in_specs=[anywhere] * 2,
        out_specs=[pl.BlockSpec(memory_space=pltpu.VMEM)] * 2,
        out_shape=[pltpu.VMEM((half, WIDE), bf16)] * 2,
        scratch_shapes=[
            pltpu.VMEM((2, half), jnp.int32),
            pltpu.SemaphoreType.DMA((3,)),
        ],
        cost_estimate=pl.CostEstimate(flops=HINT, bytes_accessed=0, transcendentals=0),
        compiler_params=pltpu.CompilerParams(vmem_limit_bytes=MESSAGE_VMEM),
    )(x, positions.reshape(2, half))


def norm_rope(proj, gain, cos, sin, out_ref):
    rows = proj.shape[0]
    total = jnp.zeros((rows, HEAD), f32)
    for h in range(HEADS):
        p = proj[:, h * HEAD : (h + 1) * HEAD]
        total = total + p * p
    inv = lax.rsqrt(jnp.sum(total, axis=1, keepdims=True) * (1.0 / D) + epsilon)
    for h in range(HEADS):
        at = slice(h * HEAD, (h + 1) * HEAD)
        y = proj[:, at] * inv * gain[:, at]
        out_ref[:, at] = (y * cos + pltpu.roll(y, HEAD // 2, 1) * sin).astype(bf16)


def project_kernel(with_q, n_ids, *refs):
    x_refs, id_refs, (shift, scale, gains, rates, w) = refs[:2], refs[2 : 2 + n_ids], refs[2 + n_ids : 7 + n_ids]
    outs, (normed, proj) = refs[7 + n_ids : -2], refs[-2:]
    at, angles = 0, []
    for x_ref, ids in zip(x_refs, id_refs or x_refs):
        rows = x_ref.shape[0]
        x = x_ref[:, :D].astype(f32)
        inv = lax.rsqrt(jnp.sum(x * x, axis=1, keepdims=True) * (1.0 / D) + epsilon)
        normed[pl.ds(at, rows), :] = (x * inv * (1.0 + scale[...]) + shift[...]).astype(bf16)
        digits = ids[:, D:].astype(f32)
        angles.append((digits[:, n_ids : n_ids + 1] * 32.0 + digits[:, n_ids + 1 : n_ids + 2]) * rates[0:1, :])
        at += rows
    angles = jnp.concatenate(angles, axis=0)
    cos, sin = jnp.cos(angles), jnp.sin(angles) * rates[1:2, :]
    names = ["q", "k", "v"] if with_q else ["k", "v"]
    out_of = dict(zip(names, outs))
    first = {"q": 0, "k": TILES, "v": 2 * TILES}
    for g, name in enumerate(["k", "q", "v"] if with_q else ["k", "v"]):
        for t in range(TILES):
            at = slice(t * TILE, (t + 1) * TILE)
            col = (first[name] + t) * TILE
            acc = jnp.dot(normed[...], w[:, col : col + TILE], preferred_element_type=f32)
            if name == "v":
                out_of[name][:, at] = acc.astype(bf16)
            else:
                proj[g, :, at] = acc
        if name != "v":
            row = 1 if name == "k" else 0
            norm_rope(proj.at[g], gains[row : row + 1, :], cos, sin, out_of[name])


def project(xs, ids, shift, scale, gains, rates, w_qkv, with_q):
    rows = sum(x.shape[0] for x in xs)
    groups = 3 if with_q else 2
    vm = pl.BlockSpec(memory_space=pltpu.VMEM)
    return pl.pallas_call(
        functools.partial(project_kernel, with_q, len(ids)),
        in_specs=[vm] * (7 + len(ids)),
        out_specs=[vm] * groups,
        out_shape=[pltpu.VMEM((rows, D), bf16)] * groups,
        scratch_shapes=[pltpu.VMEM((rows, D), bf16), pltpu.VMEM((groups - 1, rows, D), f32)],
        cost_estimate=pl.CostEstimate(
            flops=2 * rows * D * D * groups, bytes_accessed=2 * D * D * groups, transcendentals=0
        ),
        compiler_params=pltpu.CompilerParams(vmem_limit_bytes=8 << 20),
    )(*xs, *ids, shift, scale, gains, rates, w_qkv)


def merge(new, total, acc, old, old_total, old_acc):
    m = jnp.maximum(new, old)
    fade_old, fade_new = jnp.exp2(old - m), jnp.exp2(new - m)
    return m, old_total * fade_old + total * fade_new, old_acc * fade_old + acc * fade_new


def attend_kernel(n_kv, q_ref, *refs):
    kv, before, (m_ref, l_ref, acc_ref) = refs[: 2 * n_kv], refs[2 * n_kv : -3], refs[-3:]
    rows = q_ref.shape[0]
    for h in range(HEADS):
        at = slice(h * HEAD, (h + 1) * HEAD)
        q = q_ref[:, at]
        scores = [
            lax.dot_general(q, kv[2 * j][:, at], (((1,), (1,)), ((), ())), preferred_element_type=f32)
            for j in range(n_kv)
        ]
        top = scores[0]
        for s in scores[1:]:
            top = jnp.maximum(top, s)
        m = jnp.max(top, axis=1, keepdims=True) * EXP_SCALE
        total = jnp.zeros((rows, 1), f32)
        acc = jnp.zeros((rows, HEAD), f32)
        for j in range(n_kv):
            p = jnp.exp2(scores[j] * EXP_SCALE - m)
            total = total + jnp.sum(p, axis=1, keepdims=True)
            acc = acc + jnp.dot(p.astype(bf16), kv[2 * j + 1][:, at], preferred_element_type=f32)
        m = jnp.broadcast_to(m, (rows, HEAD))
        total = jnp.broadcast_to(total, (rows, HEAD))
        if before:
            m, total, acc = merge(m, total, acc, before[0][h], before[1][h], before[2][:, at])
        m_ref[h] = m
        l_ref[h] = total
        acc_ref[:, at] = acc


def attend(q, kvs, before=()):
    rows = q.shape[0]
    keys = sum(k.shape[0] for k, _ in kvs)
    flat = [a for pair in kvs for a in pair]
    vm = pl.BlockSpec(memory_space=pltpu.VMEM)
    return pl.pallas_call(
        functools.partial(attend_kernel, len(kvs)),
        in_specs=[vm] * (1 + len(flat) + len(before)),
        out_specs=[vm] * 3,
        out_shape=[
            pltpu.VMEM((HEADS, rows, HEAD), f32),
            pltpu.VMEM((HEADS, rows, HEAD), f32),
            pltpu.VMEM((rows, D), f32),
        ],
        cost_estimate=pl.CostEstimate(
            flops=8 * rows * D * keys, bytes_accessed=4 * rows * D * 2, transcendentals=rows * keys * HEADS
        ),
        compiler_params=pltpu.CompilerParams(vmem_limit_bytes=12 << 20),
    )(q, *flat, *before)


def finish_kernel(theirs, times, place, q_ref, k_ref, v_ref, m_ref, l_ref, acc_ref, x_ref, gate_ref, w_ref, *refs):
    out_ref, attended = refs[0], refs[-1]
    half = out_ref.shape[0]
    which = 1 - place[0] if theirs else place[0]
    rows = pl.ds(pl.multiple_of(which * half, half), half)
    for h in range(HEADS):
        at = slice(h * HEAD, (h + 1) * HEAD)
        s = lax.dot_general(
            q_ref[rows, at], k_ref[:, at], (((1,), (1,)), ((), ())), preferred_element_type=f32
        )
        new = jnp.max(s, axis=1, keepdims=True) * EXP_SCALE
        p = jnp.exp2(s * EXP_SCALE - new)
        total = jnp.broadcast_to(jnp.sum(p, axis=1, keepdims=True), (half, HEAD))
        acc = jnp.dot(p.astype(bf16), v_ref[:, at], preferred_element_type=f32)
        new = jnp.broadcast_to(new, (half, HEAD))
        _, total, acc = merge(new, total, acc, m_ref[h, rows, :], l_ref[h, rows, :], acc_ref[rows, at])
        attended[:, at] = (acc / total).astype(bf16)
    size = jnp.full((1, TILE), times[0, 1] - times[0, 0], jnp.int32).astype(f32) / 1000.0
    for t in range(TILES):
        at = slice(t * TILE, (t + 1) * TILE)
        proj = jnp.dot(attended[...], w_ref[:, at], preferred_element_type=f32)
        inc = size * (x_ref[rows, at].astype(f32) + gate_ref[:, at] * proj)
        out_ref[:, at] = inc
        if theirs:
            refs[1][:, at] = inc.astype(bf16)


def finish(theirs, step_times, place, q, kv, state, x, gate, w_out):
    half = q.shape[0] // 2
    keys = kv[0].shape[0]
    vm = pl.BlockSpec(memory_space=pltpu.VMEM)
    outs = [pltpu.VMEM((half, D), f32)] + [pltpu.VMEM((half, D), bf16)] * theirs
    return pl.pallas_call(
        functools.partial(finish_kernel, theirs),
        in_specs=[pl.BlockSpec(memory_space=pltpu.SMEM)] * 2 + [vm] * 9,
        out_specs=[vm] * len(outs),
        out_shape=outs,
        scratch_shapes=[pltpu.VMEM((half, D), bf16)],
        cost_estimate=pl.CostEstimate(
            flops=8 * half * D * keys + 2 * half * D * D,
            bytes_accessed=2 * D * D,
            transcendentals=half * keys * HEADS,
        ),
        compiler_params=pltpu.CompilerParams(vmem_limit_bytes=12 << 20),
    )(step_times, place, q, *kv, *state, x, gate, w_out)


def here():
    step = lax.axis_index("step")
    return step & 1, (step >> 1) & 3, step >> 3


def for_each_column(place, body):
    for xx in range(4):
        pl.when(place[1] == xx)(functools.partial(body, xx))


def split_kernel(mine, got, own, *pieces):
    place = here()
    part = own.shape[0]

    def split(xx):
        for k, out in enumerate((own,) + pieces):
            at = pl.ds((xx + k) % 4 * part, part)
            out[...] = (mine[at, :] + got[at, :].astype(f32)).astype(out.dtype)

    for_each_column(place, split)


def row_kernel(own, one, two, three, out):
    out[...] = (own[...] + one[...].astype(f32) + two[...].astype(f32) + three[...].astype(f32)).astype(bf16)


def before_kernel(own, *refs):
    place = here()
    xs, ys, outs = refs[:3], refs[3:6], refs[6:]
    yy = place[2]
    outs[0][...] = jnp.zeros(own.shape, f32)
    for k in (1, 2, 3):

        @pl.when(((yy - k) & 3) < yy)
        def _(k=k):
            outs[0][...] += ys[k - 1][...].astype(f32)

    def prefix(xx):
        total = outs[0][...]
        for chip in range(4):
            outs[(chip - xx) % 4][...] = total.astype(outs[(chip - xx) % 4].dtype)
            if chip < 3:
                j = (xx - chip) % 4
                total = total + (own if j == 0 else xs[j - 1])[...].astype(f32)

    for_each_column(place, prefix)


def given_kernel(mine, *refs):
    place = here()
    pieces, given = refs[:4], refs[4]
    part = pieces[0].shape[0]

    def join(xx):
        for k in range(4):
            at = pl.ds((xx - k) % 4 * part, part)
            given[at, :] = (pieces[k][...].astype(f32) + jnp.where(place[0] == 0, mine[at, :], 0.0)).astype(bf16)

    for_each_column(place, join)


def own_half_kernel(mine, got, *refs):
    place = here()
    pieces, (out, held, sem) = refs[:4], refs[4:]
    c, xx = place[0], place[1]
    part, half = pieces[0].shape[0], held.shape[0]
    for k in range(4):
        at = pl.ds(pl.multiple_of(((xx - k) & 3) * part, part), part)
        held[at, :] = pieces[k][...].astype(f32) + mine[at, :] + jnp.where(c == 0, 0.0, got[at, :].astype(f32))
    store = pltpu.make_async_copy(held, out.at[pl.ds(pl.multiple_of(c * half, half), half), :], sem)
    store.start()
    store.wait()


def other_half_kernel(theirs, other, begun, out, held, sem):
    place = here()
    half = held.shape[0]
    held[...] = other[...].astype(f32) + theirs[...]
    at = pl.multiple_of((1 - place[0]) * half, half)
    store = pltpu.make_async_copy(held, out.at[pl.ds(at, half), :], sem)
    store.start()
    store.wait()


def store_call(kernel, args, begun, rows):
    vm, anywhere = pl.BlockSpec(memory_space=pltpu.VMEM), pl.BlockSpec(memory_space=pl.ANY)
    return pl.pallas_call(
        kernel,
        in_specs=[vm] * len(args) + [anywhere] * len(begun),
        out_specs=anywhere,
        out_shape=jax.ShapeDtypeStruct((rows, D), f32),
        scratch_shapes=[pltpu.VMEM((rows // 2, D), f32), pltpu.SemaphoreType.DMA],
        input_output_aliases={len(args): 0} if begun else {},
        cost_estimate=pl.CostEstimate(flops=0, bytes_accessed=6 * rows * D, transcendentals=0),
        compiler_params=pltpu.CompilerParams(vmem_limit_bytes=4 << 20),
    )(*args, *begun)


def small_call(kernel, args, outs):
    vm = pl.BlockSpec(memory_space=pltpu.VMEM)
    return pl.pallas_call(
        kernel,
        in_specs=[vm] * len(args),
        out_specs=[vm] * len(outs),
        out_shape=outs,
        compiler_params=pltpu.CompilerParams(vmem_limit_bytes=3 << 20),
    )(*args)


def scan_steps(mine, theirs, sent):
    half = mine.shape[0]
    part = half // 4
    pair = [(i, i ^ 1) for i in range(32)]
    ring = range(4)

    def along_x(k):
        return [((y * 4 + x) * 2 + c, (y * 4 + (x + k) % 4) * 2 + c) for y in ring for x in ring for c in (0, 1)]

    def along_y(k):
        return [((y * 4 + x) * 2 + c, ((y + k) % 4 * 4 + x) * 2 + c) for y in ring for x in ring for c in (0, 1)]

    narrow, wide = pltpu.VMEM((part, D), bf16), pltpu.VMEM((part, D), f32)
    got = lax.ppermute(sent, "step", pair)
    own, *pieces = small_call(split_kernel, (mine, got), [wide] + [narrow] * 3)
    xs = [lax.ppermute(piece, "step", along_x(k)) for k, piece in zip((1, 2, 3), pieces)]
    (row,) = small_call(row_kernel, (own, *xs), [narrow])
    ys = [lax.ppermute(row, "step", along_y(k)) for k in (1, 2, 3)]
    home, *away = small_call(before_kernel, (own, *xs, *ys), [wide] + [narrow] * 3)
    back = [lax.ppermute(piece, "step", along_x(k)) for k, piece in zip((1, 2, 3), away)]
    (given,) = small_call(given_kernel, (mine, home, *back), [pltpu.VMEM((half, D), bf16)])
    other = lax.ppermute(given, "step", pair)
    begun = store_call(own_half_kernel, (mine, got, home, *back), (), 2 * half)
    return store_call(other_half_kernel, (theirs, other), (begun,), 2 * half)


def on_device(states, step_times, positions, w_qkv, qk_gain, w_out, time_weight):
    n = lax.axis_size("seq")
    right = [(i, (i + 1) % n) for i in range(n)]
    left = [(i, (i - 1) % n) for i in range(n)]
    to_right = lambda v: lax.ppermute(v, "seq", right)
    to_left = lambda v: lax.ppermute(v, "seq", left)
    step = lax.axis_index("step")
    place = jnp.stack([step % 2, (step // 2) % 4, step // 8])

    x = states[0]
    first, second = with_positions(x, positions)
    r_first, l_second = to_right(first), to_left(second)
    modulated = modulation(step_times, time_weight, first, second)
    shift, scale, gate, rates, bare_first, bare_second, place = lax.optimization_barrier((*modulated, place))
    r_second, l_first = to_right(bare_second), to_left(bare_first)
    forward = to_right(r_first), to_left(l_second)

    given = (shift, scale, qk_gain, rates, w_qkv)
    q, k, v = project((first, second), (), *given, True)
    near = project((r_first, l_second), (), *given, False)
    next_near = project((r_second, l_first), (r_first, l_second), *given, False)
    far = project(forward, (), *given, False)
    state = attend(q, [next_near], attend(q, [(k, v), near]))
    late = (step_times, place, q, far, state, x, gate, w_out)
    theirs, sent = finish(True, *late)
    (mine,) = finish(False, *late)
    return scan_steps(mine, theirs, sent)[None]


def solution(mesh):
    placed = (P("step", "seq", None), P("step", None), P("seq"), P(), P(), P(), P())
    return jax.shard_map(
        on_device, mesh=mesh, in_specs=placed, out_specs=P("step", "seq", None), check_vma=False
    )
```

```python
import functools
import math

import jax
import jax.numpy as jnp
from jax import lax
from jax.experimental import pallas as pl
from jax.experimental.pallas import tpu as pltpu
from jax.sharding import PartitionSpec as P

D = 1536
HEAD = 128
HEADS = D // HEAD
TILE = 512
TILES = D // TILE
MESSAGE_VMEM = 63 << 20
HINT = 1 << 33
WIDE = D + HEAD
VMEM = 16 << 20
epsilon = 1e-06
EXP_SCALE = HEAD ** (-0.5) * math.log2(math.e)
f32, bf16 = jnp.float32, jnp.bfloat16


def modulation_kernel(times, weight, first, second, shift, scale, gate, rates, bare_first, bare_second):
    rows, freq = 16, HEAD
    bare_first[...] = first[:, :D]
    bare_second[...] = second[:, :D]
    lane = lax.broadcasted_iota(jnp.int32, (rows, freq), 1)
    row = lax.broadcasted_iota(jnp.int32, (rows, 2 * freq), 0)
    t = jnp.full((rows, freq), times[0, 0], jnp.int32).astype(f32)
    angles = t * jnp.exp(-math.log(10000.0) * lane.astype(f32) / freq)
    embedded = jnp.concatenate([jnp.cos(angles), jnp.sin(angles)], axis=1)
    high = embedded.astype(bf16).astype(f32)
    middle = (embedded - high).astype(bf16).astype(f32)
    low = embedded - high - middle
    terms = jnp.where(row == 0, high, jnp.where(row == 1, middle, jnp.where(row == 2, low, 0.0))).astype(bf16)
    for g, out in enumerate((shift, scale, gate)):
        product = jnp.dot(terms, weight[:, g * D : (g + 1) * D], preferred_element_type=f32)
        out[...] = jnp.sum(product, axis=0, keepdims=True)
    half_width = HEAD // 2
    lane = lax.broadcasted_iota(jnp.int32, (1, HEAD), 1)
    rates[0:1, :] = jnp.exp(-math.log(10000.0) * (lane & (half_width - 1)).astype(f32) / half_width)
    rates[1:2, :] = jnp.where(lane < half_width, -1.0, 1.0)
    rates[2:3, :] = jnp.full((1, HEAD), times[0, 1] - times[0, 0], jnp.int32).astype(f32) / 1000.0


def modulation(step_times, time_weight, first, second):
    half = first.shape[0]
    vm = pl.BlockSpec(memory_space=pltpu.VMEM)
    return pl.pallas_call(
        modulation_kernel,
        in_specs=[pl.BlockSpec(memory_space=pltpu.SMEM), vm, vm, vm],
        out_specs=[vm] * 6,
        out_shape=[pltpu.VMEM((1, D), f32)] * 3 + [pltpu.VMEM((3, HEAD), f32)] + [pltpu.VMEM((half, D), bf16)] * 2,
        cost_estimate=pl.CostEstimate(flops=HINT, bytes_accessed=0, transcendentals=0),
        compiler_params=pltpu.CompilerParams(vmem_limit_bytes=3 << 20),
    )(step_times, time_weight, first, second)


def message_kernel(x, positions_any, first, second, positions, sems):
    rows = first.shape[0]
    ids_load = pltpu.make_async_copy(positions_any, positions, sems.at[2])
    ids_load.start()
    copies = [
        pltpu.make_async_copy(x.at[pl.ds(j * rows, rows), :], out.at[:, pl.ds(0, D)], sems.at[j])
        for j, out in enumerate((first, second))
    ]
    for copy in copies:
        copy.start()
    lane = lax.broadcasted_iota(jnp.int32, (rows, HEAD), 1)
    row = lax.broadcasted_iota(jnp.int32, (rows, HEAD), 0)
    ids_load.wait()
    digits = []
    for j in range(2):
        spread = jnp.where(row == lane, positions[j : j + 1, :], 0).astype(f32)
        ids = jnp.sum(spread, axis=1, keepdims=True).astype(jnp.int32)
        digits.append((ids >> 5, ids & 31))
    for j, out in enumerate((first, second)):
        mine, others = digits[j], digits[1 - j]
        four = jnp.where(lane == 2, others[0], jnp.where(lane == 3, others[1], 0))
        four = jnp.where(lane == 0, mine[0], jnp.where(lane == 1, mine[1], four))
        out[:, D:] = four.astype(f32).astype(bf16)
    for copy in copies:
        copy.wait()


def with_positions(x, positions):
    half = x.shape[0] // 2
    anywhere = pl.BlockSpec(memory_space=pl.ANY)
    return pl.pallas_call(
        message_kernel,
        in_specs=[anywhere] * 2,
        out_specs=[pl.BlockSpec(memory_space=pltpu.VMEM)] * 2,
        out_shape=[pltpu.VMEM((half, WIDE), bf16)] * 2,
        scratch_shapes=[
            pltpu.VMEM((2, half), jnp.int32),
            pltpu.SemaphoreType.DMA((3,)),
        ],
        cost_estimate=pl.CostEstimate(flops=HINT, bytes_accessed=0, transcendentals=0),
        compiler_params=pltpu.CompilerParams(vmem_limit_bytes=MESSAGE_VMEM),
    )(x, positions.reshape(2, half))


def norm_rope(proj, gain, cos, sin, out_ref):
    rows = proj.shape[0]
    total = jnp.zeros((rows, HEAD), f32)
    for h in range(HEADS):
        p = proj[:, h * HEAD : (h + 1) * HEAD]
        total = total + p * p
    inv = lax.rsqrt(jnp.sum(total, axis=1, keepdims=True) * (1.0 / D) + epsilon)
    for h in range(HEADS):
        at = slice(h * HEAD, (h + 1) * HEAD)
        y = proj[:, at] * inv * gain[:, at]
        out_ref[:, at] = (y * cos + pltpu.roll(y, HEAD // 2, 1) * sin).astype(bf16)


def project_kernel(with_q, n_ids, *refs):
    x_refs, id_refs, (shift, scale, gains, rates, w) = refs[:2], refs[2 : 2 + n_ids], refs[2 + n_ids : 7 + n_ids]
    outs, (normed, proj) = refs[7 + n_ids : -2], refs[-2:]
    at, angles = 0, []
    for x_ref, ids in zip(x_refs, id_refs or x_refs):
        rows = x_ref.shape[0]
        x = x_ref[:, :D].astype(f32)
        inv = lax.rsqrt(jnp.sum(x * x, axis=1, keepdims=True) * (1.0 / D) + epsilon)
        normed[pl.ds(at, rows), :] = (x * inv * (1.0 + scale[...]) + shift[...]).astype(bf16)
        digits = ids[:, D:].astype(f32)
        angles.append((digits[:, n_ids : n_ids + 1] * 32.0 + digits[:, n_ids + 1 : n_ids + 2]) * rates[0:1, :])
        at += rows
    angles = jnp.concatenate(angles, axis=0)
    cos, sin = jnp.cos(angles), jnp.sin(angles) * rates[1:2, :]
    names = ["q", "k", "v"] if with_q else ["k", "v"]
    out_of = dict(zip(names, outs))
    first = {"q": 0, "k": TILES, "v": 2 * TILES}
    for g, name in enumerate(["k", "q", "v"] if with_q else ["k", "v"]):
        for t in range(TILES):
            at = slice(t * TILE, (t + 1) * TILE)
            col = (first[name] + t) * TILE
            acc = jnp.dot(normed[...], w[:, col : col + TILE], preferred_element_type=f32)
            if name == "v":
                out_of[name][:, at] = acc.astype(bf16)
            else:
                proj[g, :, at] = acc
        if name != "v":
            row = 1 if name == "k" else 0
            norm_rope(proj.at[g], gains[row : row + 1, :], cos, sin, out_of[name])


def project(xs, ids, shift, scale, gains, rates, w_qkv, with_q):
    rows = sum(x.shape[0] for x in xs)
    groups = 3 if with_q else 2
    vm = pl.BlockSpec(memory_space=pltpu.VMEM)
    return pl.pallas_call(
        functools.partial(project_kernel, with_q, len(ids)),
        in_specs=[vm] * (7 + len(ids)),
        out_specs=[vm] * groups,
        out_shape=[pltpu.VMEM((rows, D), bf16)] * groups,
        scratch_shapes=[pltpu.VMEM((rows, D), bf16), pltpu.VMEM((groups - 1, rows, D), f32)],
        cost_estimate=pl.CostEstimate(
            flops=2 * rows * D * D * groups, bytes_accessed=2 * D * D * groups, transcendentals=0
        ),
        compiler_params=pltpu.CompilerParams(vmem_limit_bytes=8 << 20),
    )(*xs, *ids, shift, scale, gains, rates, w_qkv)


def merge(new, total, acc, old, old_total, old_acc):
    m = jnp.maximum(new, old)
    fade_old, fade_new = jnp.exp2(old - m), jnp.exp2(new - m)
    return m, old_total * fade_old + total * fade_new, old_acc * fade_old + acc * fade_new


def attend_kernel(n_kv, q_ref, *refs):
    kv, before, (m_ref, l_ref, acc_ref) = refs[: 2 * n_kv], refs[2 * n_kv : -3], refs[-3:]
    rows = q_ref.shape[0]
    for h in range(HEADS):
        at = slice(h * HEAD, (h + 1) * HEAD)
        q = q_ref[:, at]
        scores = [
            lax.dot_general(q, kv[2 * j][:, at], (((1,), (1,)), ((), ())), preferred_element_type=f32)
            for j in range(n_kv)
        ]
        top = scores[0]
        for s in scores[1:]:
            top = jnp.maximum(top, s)
        m = jnp.max(top, axis=1, keepdims=True) * EXP_SCALE
        total = jnp.zeros((rows, 1), f32)
        acc = jnp.zeros((rows, HEAD), f32)
        for j in range(n_kv):
            p = jnp.exp2(scores[j] * EXP_SCALE - m)
            total = total + jnp.sum(p, axis=1, keepdims=True)
            acc = acc + jnp.dot(p.astype(bf16), kv[2 * j + 1][:, at], preferred_element_type=f32)
        m = jnp.broadcast_to(m, (rows, HEAD))
        total = jnp.broadcast_to(total, (rows, HEAD))
        if before:
            m, total, acc = merge(m, total, acc, before[0][h], before[1][h], before[2][:, at])
        m_ref[h] = m
        l_ref[h] = total
        acc_ref[:, at] = acc


def attend(q, kvs, before=()):
    rows = q.shape[0]
    keys = sum(k.shape[0] for k, _ in kvs)
    flat = [a for pair in kvs for a in pair]
    vm = pl.BlockSpec(memory_space=pltpu.VMEM)
    return pl.pallas_call(
        functools.partial(attend_kernel, len(kvs)),
        in_specs=[vm] * (1 + len(flat) + len(before)),
        out_specs=[vm] * 3,
        out_shape=[
            pltpu.VMEM((HEADS, rows, HEAD), f32),
            pltpu.VMEM((HEADS, rows, HEAD), f32),
            pltpu.VMEM((rows, D), f32),
        ],
        cost_estimate=pl.CostEstimate(
            flops=8 * rows * D * keys, bytes_accessed=4 * rows * D * 2, transcendentals=rows * keys * HEADS
        ),
        compiler_params=pltpu.CompilerParams(vmem_limit_bytes=12 << 20),
    )(q, *flat, *before)


def finish_kernel(theirs, rates, q_ref, k_ref, v_ref, m_ref, l_ref, acc_ref, x_ref, gate_ref, w_ref, *refs):
    out_ref, attended = refs[0], refs[-1]
    half = out_ref.shape[0]
    which = 1 - here()[0] if theirs else here()[0]
    rows = pl.ds(pl.multiple_of(which * half, half), half)
    for h in range(HEADS):
        at = slice(h * HEAD, (h + 1) * HEAD)
        s = lax.dot_general(
            q_ref[rows, at], k_ref[:, at], (((1,), (1,)), ((), ())), preferred_element_type=f32
        )
        new = jnp.max(s, axis=1, keepdims=True) * EXP_SCALE
        p = jnp.exp2(s * EXP_SCALE - new)
        total = jnp.broadcast_to(jnp.sum(p, axis=1, keepdims=True), (half, HEAD))
        acc = jnp.dot(p.astype(bf16), v_ref[:, at], preferred_element_type=f32)
        new = jnp.broadcast_to(new, (half, HEAD))
        _, total, acc = merge(new, total, acc, m_ref[h, rows, :], l_ref[h, rows, :], acc_ref[rows, at])
        attended[:, at] = (acc / total).astype(bf16)
    size = jnp.concatenate([rates[2:3, :]] * (TILE // HEAD), axis=1)
    for t in range(TILES):
        at = slice(t * TILE, (t + 1) * TILE)
        proj = jnp.dot(attended[...], w_ref[:, at], preferred_element_type=f32)
        inc = size * (x_ref[rows, at].astype(f32) + gate_ref[:, at] * proj)
        out_ref[:, at] = inc
        if theirs:
            refs[1][:, at] = inc.astype(bf16)


def finish(theirs, rates, q, kv, state, x, gate, w_out):
    half = q.shape[0] // 2
    keys = kv[0].shape[0]
    vm = pl.BlockSpec(memory_space=pltpu.VMEM)
    outs = [pltpu.VMEM((half, D), f32)] + [pltpu.VMEM((half, D), bf16)] * theirs
    return pl.pallas_call(
        functools.partial(finish_kernel, theirs),
        in_specs=[vm] * 10,
        out_specs=[vm] * len(outs),
        out_shape=outs,
        scratch_shapes=[pltpu.VMEM((half, D), bf16)],
        cost_estimate=pl.CostEstimate(
            flops=8 * half * D * keys + 2 * half * D * D,
            bytes_accessed=2 * D * D,
            transcendentals=half * keys * HEADS,
        ),
        compiler_params=pltpu.CompilerParams(vmem_limit_bytes=12 << 20),
    )(rates, q, *kv, *state, x, gate, w_out)


def here():
    step = lax.axis_index("step")
    return step & 1, (step >> 1) & 3, step >> 3


def for_each_column(place, body):
    for xx in range(4):
        pl.when(place[1] == xx)(functools.partial(body, xx))


def split_kernel(mine, got, own, *pieces):
    place = here()
    part = own.shape[0]

    def split(xx):
        for k, out in enumerate((own,) + pieces):
            at = pl.ds((xx + k) % 4 * part, part)
            out[...] = (mine[at, :] + got[at, :].astype(f32)).astype(out.dtype)

    for_each_column(place, split)


def row_kernel(own, one, two, three, out):
    out[...] = (own[...] + one[...].astype(f32) + two[...].astype(f32) + three[...].astype(f32)).astype(bf16)


def before_kernel(own, *refs):
    place = here()
    xs, ys, outs = refs[:3], refs[3:6], refs[6:]
    yy = place[2]
    outs[0][...] = jnp.zeros(own.shape, f32)
    for k in (1, 2, 3):

        @pl.when(((yy - k) & 3) < yy)
        def _(k=k):
            outs[0][...] += ys[k - 1][...].astype(f32)

    def prefix(xx):
        total = outs[0][...]
        for chip in range(4):
            outs[(chip - xx) % 4][...] = total.astype(outs[(chip - xx) % 4].dtype)
            if chip < 3:
                j = (xx - chip) % 4
                total = total + (own if j == 0 else xs[j - 1])[...].astype(f32)

    for_each_column(place, prefix)


def given_kernel(mine, *refs):
    place = here()
    pieces, given = refs[:4], refs[4]
    part = pieces[0].shape[0]

    def join(xx):
        for k in range(4):
            at = pl.ds((xx - k) % 4 * part, part)
            given[at, :] = (pieces[k][...].astype(f32) + jnp.where(place[0] == 0, mine[at, :], 0.0)).astype(bf16)

    for_each_column(place, join)


def own_half_kernel(mine, got, *refs):
    place = here()
    pieces, (out, held, sem) = refs[:4], refs[4:]
    c, xx = place[0], place[1]
    part, half = pieces[0].shape[0], held.shape[0]
    for k in range(4):
        at = pl.ds(pl.multiple_of(((xx - k) & 3) * part, part), part)
        held[at, :] = pieces[k][...].astype(f32) + mine[at, :] + jnp.where(c == 0, 0.0, got[at, :].astype(f32))
    store = pltpu.make_async_copy(held, out.at[pl.ds(pl.multiple_of(c * half, half), half), :], sem)
    store.start()
    store.wait()


def other_half_kernel(theirs, other, begun, out, held, sem):
    place = here()
    half = held.shape[0]
    held[...] = other[...].astype(f32) + theirs[...]
    at = pl.multiple_of((1 - place[0]) * half, half)
    store = pltpu.make_async_copy(held, out.at[pl.ds(at, half), :], sem)
    store.start()
    store.wait()


def store_call(kernel, args, begun, rows):
    vm, anywhere = pl.BlockSpec(memory_space=pltpu.VMEM), pl.BlockSpec(memory_space=pl.ANY)
    return pl.pallas_call(
        kernel,
        in_specs=[vm] * len(args) + [anywhere] * len(begun),
        out_specs=anywhere,
        out_shape=jax.ShapeDtypeStruct((rows, D), f32),
        scratch_shapes=[pltpu.VMEM((rows // 2, D), f32), pltpu.SemaphoreType.DMA],
        input_output_aliases={len(args): 0} if begun else {},
        cost_estimate=pl.CostEstimate(flops=0, bytes_accessed=6 * rows * D, transcendentals=0),
        compiler_params=pltpu.CompilerParams(vmem_limit_bytes=4 << 20),
    )(*args, *begun)


def small_call(kernel, args, outs):
    vm = pl.BlockSpec(memory_space=pltpu.VMEM)
    return pl.pallas_call(
        kernel,
        in_specs=[vm] * len(args),
        out_specs=[vm] * len(outs),
        out_shape=outs,
        compiler_params=pltpu.CompilerParams(vmem_limit_bytes=3 << 20),
    )(*args)


def scan_steps(mine, theirs, sent):
    half = mine.shape[0]
    part = half // 4
    pair = [(i, i ^ 1) for i in range(32)]
    ring = range(4)

    def along_x(k):
        return [((y * 4 + x) * 2 + c, (y * 4 + (x + k) % 4) * 2 + c) for y in ring for x in ring for c in (0, 1)]

    def along_y(k):
        return [((y * 4 + x) * 2 + c, ((y + k) % 4 * 4 + x) * 2 + c) for y in ring for x in ring for c in (0, 1)]

    narrow, wide = pltpu.VMEM((part, D), bf16), pltpu.VMEM((part, D), f32)
    got = lax.ppermute(sent, "step", pair)
    own, *pieces = small_call(split_kernel, (mine, got), [wide] + [narrow] * 3)
    xs = [lax.ppermute(piece, "step", along_x(k)) for k, piece in zip((1, 2, 3), pieces)]
    (row,) = small_call(row_kernel, (own, *xs), [narrow])
    ys = [lax.ppermute(row, "step", along_y(k)) for k in (1, 2, 3)]
    home, *away = small_call(before_kernel, (own, *xs, *ys), [wide] + [narrow] * 3)
    back = [lax.ppermute(piece, "step", along_x(k)) for k, piece in zip((1, 2, 3), away)]
    (given,) = small_call(given_kernel, (mine, home, *back), [pltpu.VMEM((half, D), bf16)])
    other = lax.ppermute(given, "step", pair)
    begun = store_call(own_half_kernel, (mine, got, home, *back), (), 2 * half)
    return store_call(other_half_kernel, (theirs, other), (begun,), 2 * half)


def on_device(states, step_times, positions, w_qkv, qk_gain, w_out, time_weight):
    n = lax.axis_size("seq")
    right = [(i, (i + 1) % n) for i in range(n)]
    left = [(i, (i - 1) % n) for i in range(n)]
    to_right = lambda v: lax.ppermute(v, "seq", right)
    to_left = lambda v: lax.ppermute(v, "seq", left)
    x = states[0]
    first, second = with_positions(x, positions)
    r_first, l_second = to_right(first), to_left(second)
    modulated = modulation(step_times, time_weight, first, second)
    shift, scale, gate, rates, bare_first, bare_second = modulated
    r_second, l_first = to_right(bare_second), to_left(bare_first)
    forward = to_right(r_first), to_left(l_second)

    given = (shift, scale, qk_gain, rates, w_qkv)
    q, k, v = project((first, second), (), *given, True)
    near = project((r_first, l_second), (), *given, False)
    next_near = project((r_second, l_first), (r_first, l_second), *given, False)
    far = project(forward, (), *given, False)
    state = attend(q, [next_near], attend(q, [(k, v), near]))
    late = (rates, q, far, state, x, gate, w_out)
    theirs, sent = finish(True, *late)
    (mine,) = finish(False, *late)
    return scan_steps(mine, theirs, sent)[None]


def solution(mesh):
    placed = (P("step", "seq", None), P("step", None), P("seq"), P(), P(), P(), P())
    return jax.shard_map(
        on_device, mesh=mesh, in_specs=placed, out_specs=P("step", "seq", None), check_vma=False
    )
```
